256 devices in a mesh: dp: 8 (over y, core), seq: 32 (over x, z).
Axes of the slice: x: 4, y: 4, z: 8, core: 2. Of those that a mesh axis runs over, the one named last changes fastest.
Arguments:
- hidden_in: bfloat16 [8, 64, 64, 1152], P('dp', 'seq'), may hold values from -2.5 to 2.5
- spatial_qkv: bfloat16 [8, 64, 64, 3456], P('dp', 'seq'), may hold values from -6 to 6
- temporal_qkv: bfloat16 [8, 64, 64, 3456], P('dp', 'seq'), may hold values from -6 to 6
- teacher_target: bfloat16 [8, 64, 64, 1152], P('dp', 'seq'), may hold values from -5 to 5
- spatial_proj: bfloat16 [1152, 1152], P('seq'), may hold values from -0.1875 to 0.1875
- temporal_proj: bfloat16 [1152, 1152], P('seq'), may hold values from -0.1875 to 0.1875
Outputs:
- clip_loss: float32 [8], P('dp')
- spatial_qkv_grad: bfloat16 [8, 64, 64, 3456], P('dp', 'seq')
- temporal_qkv_grad: bfloat16 [8, 64, 64, 3456], P('dp', 'seq')
- spatial_proj_grad: float32 [1152, 1152], P('seq')
- temporal_proj_grad: float32 [1152, 1152], P('seq')
The draws below stay inside these ranges and needn't reach their ends.
All inputs are finite; a program needn't handle non-finite values.
Results may differ from the reference program's by a relative error of at most 0.018.
Values may be sent and summed in bfloat16 or wider, within the bound.
No kernel may reach another device: no remote copies, remote signals or barrier semaphores. Data moves between devices by JAX's collectives and lax.ppermute only.
A program may use at most 128 MiB of HBM per device.

```python
import math
import jax
import jax.numpy as jnp
from jax import lax

D = 1152
HEADS = 16
PATCHES = 64
CLIPS = 8
FRAMES = 64


def frame_rise():
    steps_along = jnp.arange(FRAMES, dtype=jnp.float32) / max(FRAMES - 1, 1)
    return jnp.exp(math.log(3.0) * steps_along).reshape(1, FRAMES, 1, 1)


def draw_hidden_in(key, part):
    key = jax.random.fold_in(key, 11)
    key_base = jax.random.fold_in(key, 0)
    full_shape = (CLIPS, FRAMES, PATCHES, D)
    values_base = jnp.clip(jax.random.normal(key_base, full_shape, jnp.float32), -4.0, 4.0)
    return (0.2 * frame_rise() * values_base).astype(jnp.bfloat16)


def draw_teacher_target(key, part):
    key = jax.random.fold_in(key, 12)
    key_base = jax.random.fold_in(key, 0)
    full_shape = (CLIPS, FRAMES, PATCHES, D)
    values_base = jnp.clip(jax.random.normal(key_base, full_shape, jnp.float32), -4.0, 4.0)
    return (0.4 * frame_rise() * values_base).astype(jnp.bfloat16)


def draw_spatial_qkv(key, part):
    key = jax.random.fold_in(key, 13)
    key_base = jax.random.fold_in(key, 0)
    full_shape = (CLIPS, FRAMES, PATCHES, 3 * D)
    values_base = jnp.clip(1.4 * jax.random.normal(key_base, full_shape, jnp.float32), -4.5, 4.5)
    return values_base.astype(jnp.bfloat16)


def draw_temporal_qkv(key, part):
    key = jax.random.fold_in(key, 14)
    key_base = jax.random.fold_in(key, 0)
    full_shape = (CLIPS, FRAMES, PATCHES, 3 * D)
    values_base = jnp.clip(1.4 * jax.random.normal(key_base, full_shape, jnp.float32), -4.5, 4.5)
    return values_base.astype(jnp.bfloat16)


def shard_levels(own_key, shape, cuts, smallest, high):
    gain = 1.0
    for dim, shards_of in cuts:
        draws = jax.random.uniform(jax.random.fold_in(jax.random.fold_in(own_key, 6), dim), (shards_of,), jnp.float32, smallest / len(cuts), high / len(cuts))
        gain = gain * jnp.repeat(jnp.exp(draws), shape[dim] // shards_of).reshape((-1,) + (1,) * (len(shape) - 1 - dim))
    return gain


def normal_values(key, shape, scale, bound, cuts=(), kind=jnp.bfloat16):
    gain = shard_levels(key, shape, cuts, -0.22, 0.18) if cuts else 1.0
    array = jax.random.normal(key, shape, jnp.float32) * scale * gain
    return jnp.minimum(jnp.maximum(array, -bound), bound).astype(kind)


def setup_inputs(seed: int = 0) -> dict:
    splits = jax.random.split(jax.random.key(seed), 7)
    hidden_in = draw_hidden_in(jax.random.fold_in(splits[6], 71), 0)
    spatial_qkv = draw_spatial_qkv(jax.random.fold_in(splits[6], 71), 0)
    temporal_qkv = draw_temporal_qkv(jax.random.fold_in(splits[6], 71), 0)
    teacher_target = draw_teacher_target(jax.random.fold_in(splits[6], 71), 0)
    spatial_proj = normal_values(splits[4], (D, D), D ** -0.5, 0.1875, ((0, 32),))
    temporal_proj = normal_values(splits[5], (D, D), D ** -0.5, 0.1875, ((0, 32),))
    return dict(hidden_in=hidden_in, spatial_qkv=spatial_qkv, temporal_qkv=temporal_qkv, teacher_target=teacher_target, spatial_proj=spatial_proj, temporal_proj=temporal_proj)


huber_delta = 0.03

def product(form, left, right):
    return jnp.einsum(form, left.astype(jnp.float32), right.astype(jnp.float32))

def split_qkv(packed):
    channels = packed.shape[-1] // 3
    heads_split = packed.reshape(packed.shape[:-1] + (3, HEADS, channels // HEADS))
    return (heads_split[..., 0, :, :], heads_split[..., 1, :, :], heads_split[..., 2, :, :])

def attend(packed):
    queries, key_rows, values = split_qkv(packed)
    scaling = queries.shape[-1] ** (-0.5)
    scores = product('nqhe,nkhe->nhqk', queries, key_rows) * scaling
    attn_probs = jax.nn.softmax(scores, axis=-1)
    rounded = attn_probs.astype(jnp.bfloat16)
    mixed = product('nhqk,nkhe->nqhe', rounded, values).astype(jnp.bfloat16)
    return (attn_probs, rounded, mixed.reshape(packed.shape[:-1] + (packed.shape[-1] // 3,)))

def attend_back(packed, attn_probs, rounded, mix_grad):
    queries, key_rows, values = split_qkv(packed)
    scaling = queries.shape[-1] ** (-0.5)
    out_heads = mix_grad.reshape(queries.shape)
    value_grad = product('nhqk,nqhe->nkhe', rounded, out_heads)
    prob_grad = product('nqhe,nkhe->nhqk', out_heads, values)
    inner = lax.optimization_barrier(jnp.sum(prob_grad * attn_probs, axis=-1, keepdims=True))
    score_grad = (attn_probs * (prob_grad - inner) * scaling).astype(jnp.bfloat16)
    query_grad = product('nhqk,nkhe->nqhe', score_grad, key_rows)
    key_grad = product('nhqk,nqhe->nkhe', score_grad, queries)
    joined = jnp.stack([query_grad, key_grad, value_grad], axis=-3).astype(jnp.bfloat16)
    return joined.reshape(packed.shape)

def reference(hidden_in, spatial_qkv, temporal_qkv, teacher_target, spatial_proj, temporal_proj):
    cell_count = FRAMES * PATCHES * D

    def one_clip(pieces):
        field, space_packed, time_packed, target = pieces
        space_probs, space_round, spatial_mix = attend(space_packed)
        time_by_patch = jnp.swapaxes(time_packed, 0, 1)
        time_probs, time_round, time_mix_patch = attend(time_by_patch)
        temporal_mix = jnp.swapaxes(time_mix_patch, 0, 1)
        after = field.astype(jnp.float32) + product('fpd,de->fpe', spatial_mix, spatial_proj)
        output = after + product('fpd,de->fpe', temporal_mix, temporal_proj)
        resid = output - target.astype(jnp.float32)
        spread = jnp.sqrt(jnp.sum(resid * resid) / cell_count + huber_delta ** 2)
        loss_value = spread - huber_delta
        out_grad = (resid / spread).astype(jnp.bfloat16)
        space_weight = product('fpd,fpe->de', spatial_mix, out_grad)
        time_weight = product('fpd,fpe->de', temporal_mix, out_grad)
        time_mix_grad = product('fpe,de->fpd', out_grad, temporal_proj).astype(jnp.bfloat16)
        space_mix_grad = product('fpe,de->fpd', out_grad, spatial_proj).astype(jnp.bfloat16)
        time_grad = attend_back(time_by_patch, time_probs, time_round, jnp.swapaxes(time_mix_grad, 0, 1))
        time_grad = jnp.swapaxes(time_grad, 0, 1)
        space_grad = attend_back(space_packed, space_probs, space_round, space_mix_grad)
        return (loss_value, space_grad, time_grad, space_weight, time_weight)
    losses, space_grads, time_grads, space_weights, time_weights = lax.map(one_clip, (hidden_in, spatial_qkv, temporal_qkv, teacher_target))
    return (losses, space_grads, time_grads, lax.optimization_barrier(jnp.sum(space_weights, axis=0)), lax.optimization_barrier(jnp.sum(time_weights, axis=0)))
```

```python
import functools

import jax
import jax.numpy as jnp
from jax import lax
from jax.experimental import pallas as pl
from jax.experimental.pallas import tpu as pltpu
from jax.sharding import Mesh, PartitionSpec as P

HEADS = 16
D = 1152
E = D // HEADS
TOKENS = 128
LANES = 128
SEQ = ("x", "z")
DP = ("y", "core")
HUBER_DELTA = 0.03
CELLS = 64 * 64 * D
SCALING = E ** (-0.5)
BF16 = jnp.bfloat16
F32 = jnp.float32
VMEM_BYTES = 48 * 1024 * 1024

NN = (((1,), (0,)), ((), ()))
NT = (((1,), (1,)), ((), ()))
TN = (((0,), (0,)), ((), ()))


def mul(left, right, dims):
    return lax.dot_general(left, right, dims, preferred_element_type=F32)


def window(head):
    low = E * head // LANES
    high = (E * head + E - 1) // LANES + 1
    return low * LANES, high * LANES


def head_mask(head, low, high):
    lane = lax.broadcasted_iota(jnp.int32, (TOKENS, high - low), 1) + low
    return jnp.where((lane >= E * head) & (lane < E * head + E), 1.0, 0.0).astype(BF16)


def same_sequence(temporal):
    row = lax.broadcasted_iota(jnp.int32, (TOKENS, TOKENS), 0)
    col = lax.broadcasted_iota(jnp.int32, (TOKENS, TOKENS), 1)
    if temporal:
        return (row & 1) == (col & 1)
    return (row >> 6) == (col >> 6)


def natural_from_sent():
    nat = lax.broadcasted_iota(jnp.int32, (TOKENS, TOKENS), 0)
    sent = lax.broadcasted_iota(jnp.int32, (TOKENS, TOKENS), 1)
    goes = ((sent >> 1) & 1) * 64 + (sent >> 2) * 2 + (sent & 1)
    return jnp.where(nat == goes, 1.0, 0.0).astype(BF16)


class Tiles:
    def __init__(self, ref, offset, scale=None):
        self.ref, self.offset, self.scale, self.pending = ref, offset, scale, None

    def add(self, head, value):
        low, high = window(head)
        for tile in range(low, high, LANES):
            part = value[:, tile - low : tile - low + LANES]
            if E * head > tile:
                part = self.pending + part
            if E * head + E >= tile + LANES:
                if self.scale is not None:
                    part = part * self.scale
                at = self.offset + tile
                self.ref[:, at : at + LANES] = part.astype(self.ref.dtype)
            else:
                self.pending = part


def attend_kernel(temporal, x_ref, mix_ref, probs_ref):
    same = same_sequence(temporal)
    out = Tiles(mix_ref, 0)
    for head in range(HEADS):
        low, high = window(head)
        mask = head_mask(head, low, high)
        queries = x_ref[:, low:high]
        keys = x_ref[:, D + low : D + high] * mask
        values = x_ref[:, 2 * D + low : 2 * D + high] * mask
        scores = jnp.where(same, mul(queries, keys, NT) * SCALING, -1e30)
        powers = jnp.exp(scores - jnp.max(scores, axis=1, keepdims=True))
        probs = powers / jnp.sum(powers, axis=1, keepdims=True)
        probs_ref[head] = probs
        out.add(head, mul(probs.astype(BF16), values, NN))


def attend(x, temporal):
    return pl.pallas_call(
        functools.partial(attend_kernel, temporal),
        out_shape=(
            jax.ShapeDtypeStruct((TOKENS, D), BF16),
            jax.ShapeDtypeStruct((HEADS, TOKENS, TOKENS), F32),
        ),
        compiler_params=pltpu.CompilerParams(vmem_limit_bytes=VMEM_BYTES),
        name="attend_time" if temporal else "attend_space",
    )(x)


def attend_back_kernel(inv_ref, x_ref, probs_ref, grad_ref, out_ref):
    inv = inv_ref[0]
    query_out = Tiles(out_ref, 0)
    key_out = Tiles(out_ref, D)
    value_out = Tiles(out_ref, 2 * D, inv)
    for head in range(HEADS):
        low, high = window(head)
        mask = head_mask(head, low, high)
        queries = x_ref[:, low:high] * mask
        keys = x_ref[:, D + low : D + high] * mask
        values = x_ref[:, 2 * D + low : 2 * D + high]
        grads = grad_ref[:, low:high] * mask
        probs = probs_ref[head]
        value_out.add(head, mul(probs.astype(BF16), grads, TN))
        prob_grad = mul(grads, values, NT)
        inner = jnp.sum(prob_grad * probs, axis=1, keepdims=True)
        score_grad = (probs * (prob_grad - inner) * (SCALING * inv)).astype(BF16)
        query_out.add(head, mul(score_grad, keys, NN))
        key_out.add(head, mul(score_grad, queries, TN))


def attend_back(inv, x, probs, grad, name):
    vmem = pl.BlockSpec(memory_space=pltpu.VMEM)
    return pl.pallas_call(
        attend_back_kernel,
        out_shape=jax.ShapeDtypeStruct((TOKENS, 3 * D), BF16),
        in_specs=[pl.BlockSpec(memory_space=pltpu.SMEM), vmem, vmem, vmem],
        compiler_params=pltpu.CompilerParams(vmem_limit_bytes=VMEM_BYTES),
        name=name,
    )(inv, x, probs, grad)


def project_kernel(place_ref, hidden_ref, target_ref, space_ref, time_ref, *rest):
    own_refs, other_refs = rest[0:4], rest[4:8]
    resid_ref, space_grad_ref, time_grad_ref, time_mix_ref = rest[8:12]
    weights, sems = rest[12:]
    at_x, at_core = place_ref[0], place_ref[1]
    copies = []
    for k in range(4):
        rows = pl.ds(pl.multiple_of(lax.rem(at_x + 4 - k, 4) * 288, 288), 288)
        for n, (refs, which) in enumerate(((own_refs, at_core), (other_refs, 1 - at_core))):
            copy = pltpu.make_async_copy(refs[k], weights.at[which, rows], sems.at[2 * k + n])
            copy.start()
            copies.append(copy)
    natural = natural_from_sent()
    time_mix = mul(natural, time_ref[...], NN).astype(BF16)
    time_mix_ref[...] = time_mix
    base = hidden_ref[...].astype(F32) - target_ref[...].astype(F32)
    for copy in copies:
        copy.wait()
    resid = (
        base
        + mul(space_ref[...], weights[0], NN)
        + mul(time_mix, weights[1], NN)
    )
    total = jnp.sum(resid * resid)
    out_grad = resid.astype(BF16)
    resid_ref[...] = out_grad
    time_grad = mul(out_grad, weights[1], NT).astype(BF16)
    time_grad_ref[:, :D] = mul(natural, time_grad, TN).astype(BF16)
    lane = lax.broadcasted_iota(jnp.int32, (TOKENS, LANES), 1)
    whole = jnp.full((TOKENS, LANES), total, F32)
    first = whole.astype(BF16).astype(F32)
    second = (whole - first).astype(BF16).astype(F32)
    third = whole - first - second
    parts = jnp.where(lane == 0, first, jnp.where(lane == 1, second, jnp.where(lane == 2, third, 0.0)))
    time_grad_ref[:, D:] = parts.astype(BF16)
    space_grad_ref[...] = mul(out_grad, weights[0], NT).astype(BF16)


def project(place, hidden, target, space_mix, time_mix, own, other):
    vmem = pl.BlockSpec(memory_space=pltpu.VMEM)
    rows = jax.ShapeDtypeStruct((TOKENS, D), BF16)
    return pl.pallas_call(
        project_kernel,
        out_shape=(rows, rows, jax.ShapeDtypeStruct((TOKENS, D + LANES), BF16), rows),
        in_specs=[pl.BlockSpec(memory_space=pltpu.SMEM)]
        + [vmem] * 4
        + [pl.BlockSpec(memory_space=pl.ANY)] * 8,
        scratch_shapes=[pltpu.VMEM((2, D, D), BF16), pltpu.SemaphoreType.DMA((8,))],
        compiler_params=pltpu.CompilerParams(vmem_limit_bytes=VMEM_BYTES),
        name="project",
    )(place, hidden, target, space_mix, time_mix, *own, *other)


def choose_kernel(space_ref, time_ref, out_ref):
    for part in range(4):
        col = lax.broadcasted_iota(jnp.int32, (D, 288), 0)
        to = lax.broadcasted_iota(jnp.int32, (D, 288), 1)
        block = (to * 7282) >> 16
        wanted = block * 36 + part * 9 + (to - block * 9)
        chosen = jnp.where(col == wanted, 1.0, 0.0).astype(BF16)
        out_ref[2 * part] = mul(space_ref[...], chosen, NN).astype(BF16)
        out_ref[2 * part + 1] = mul(time_ref[...], chosen, NN).astype(BF16)


def choose(space_mix, time_mix):
    return pl.pallas_call(
        choose_kernel,
        out_shape=jax.ShapeDtypeStruct((8, TOKENS, 288), BF16),
        compiler_params=pltpu.CompilerParams(vmem_limit_bytes=VMEM_BYTES),
        name="choose",
    )(space_mix, time_mix)


def weight_kernel(place_ref, inv_ref, mix_ref, own_ref, other_ref, out_ref, total):
    at_x, at_core, at_y = place_ref[0], place_ref[1], place_ref[2]
    for k in range(4):
        from_y = lax.rem(at_y + 4 - k, 4)
        for refs, which in ((own_ref, at_core), (other_ref, 1 - at_core)):
            clip = 2 * from_y + which
            out_grad = (refs[k].astype(F32) * inv_ref[clip]).astype(BF16)
            term = mul(mix_ref[clip], out_grad, TN)
            if k == 0 and refs is own_ref:
                total[...] = term
            else:
                total[...] += term
    for k in range(4):
        rows = pl.ds(pl.multiple_of(lax.rem(at_x + k, 4) * 72, 72), 72)
        out_ref[k] = total[rows, :].astype(BF16)


def weight_grad(place, inv, mixes, own, other):
    vmem = pl.BlockSpec(memory_space=pltpu.VMEM)
    smem = pl.BlockSpec(memory_space=pltpu.SMEM)
    return pl.pallas_call(
        weight_kernel,
        out_shape=jax.ShapeDtypeStruct((4, 72, D), BF16),
        in_specs=[smem, smem, vmem, vmem, vmem],
        scratch_shapes=[pltpu.VMEM((288, D), F32)],
        compiler_params=pltpu.CompilerParams(vmem_limit_bytes=VMEM_BYTES),
        name="weight_grad",
    )(place, inv, mixes, own, other)


def shift(value, axis, size, step):
    return lax.ppermute(value, axis, [(i, (i + step) % size) for i in range(size)])


def swap(value):
    return lax.ppermute(value, "core", [(0, 1), (1, 0)])


def exchange(value, axis):
    return lax.all_to_all(value, axis, split_axis=0, concat_axis=0, tiled=True)


def per_device(hidden_in, spatial_qkv, temporal_qkv, teacher_target, spatial_proj, temporal_proj):
    at_x, at_core, at_y = (lax.axis_index(a) for a in ("x", "core", "y"))
    place = jnp.stack([at_x, at_core, at_y]).astype(jnp.int32)

    sent = temporal_qkv.reshape(2, 32, 2, 3 * D).transpose(1, 0, 2, 3).reshape(32, 4, 3 * D)
    time_x = exchange(sent, SEQ).reshape(TOKENS, 3 * D)

    rows = jnp.where(at_core == 0, spatial_proj, temporal_proj)
    gathered = exchange(jnp.broadcast_to(rows[None], (8, 36, D)), "z").reshape(288, D)
    own = [gathered] + [shift(gathered, "x", 4, k) for k in (1, 2, 3)]
    other = [swap(block) for block in own]

    space_x = spatial_qkv.reshape(TOKENS, 3 * D)
    space_mix, space_probs = attend(space_x, False)
    time_mix_sent, time_probs = attend(time_x, True)
    time_mix = exchange(time_mix_sent.reshape(32, 4, D), SEQ).reshape(TOKENS, D)

    resid, space_grad, time_grad, time_mix = project(
        place,
        hidden_in.reshape(TOKENS, D),
        teacher_target.reshape(TOKENS, D),
        space_mix,
        time_mix,
        own,
        other,
    )
    time_back = exchange(time_grad.reshape(32, 4, D + LANES), SEQ)

    resids = jnp.stack([resid] + [shift(resid, "y", 4, k) for k in (1, 2, 3)])
    resids_other = swap(resids)
    mixes = exchange(choose(space_mix, time_mix), DP)

    total = jnp.sum(time_back[:, 0, D : D + 3].astype(F32))
    spread = jnp.sqrt(total / CELLS + HUBER_DELTA**2)
    clip_loss = (spread - HUBER_DELTA).reshape(1)
    inv = (1.0 / spread).reshape(1)
    invs = exchange(jnp.broadcast_to(inv, (8, 1, LANES)), DP)[:, 0, 0]

    time_out = attend_back(
        inv, time_x, time_probs, time_back.reshape(TOKENS, D + LANES), "attend_back_time"
    )
    time_out = exchange(time_out.reshape(32, 4, 3 * D), SEQ)
    temporal_qkv_grad = time_out.reshape(32, 2, 2, 3 * D).transpose(1, 0, 2, 3)

    spatial_qkv_grad = attend_back(inv, space_x, space_probs, space_grad, "attend_back_space")

    partial = weight_grad(place, invs, mixes, resids, resids_other)
    summed = sum(
        [partial[0].astype(F32)] + [shift(partial[k], "x", 4, k).astype(F32) for k in (1, 2, 3)]
    ).astype(BF16)
    pieces = exchange(summed.reshape(8, 9, D), "z")
    piece = jnp.sum(pieces.astype(F32), axis=0).astype(BF16)
    blocks = exchange(jnp.broadcast_to(piece[None], (8, 9, D)), DP)
    blocks = blocks.reshape(4, 2, 9, D).astype(F32)
    return (
        clip_loss,
        spatial_qkv_grad.reshape(1, 2, 64, 3 * D),
        temporal_qkv_grad.reshape(1, 2, 64, 3 * D),
        blocks[:, 0].reshape(36, D),
        blocks[:, 1].reshape(36, D),
    )


def solution(mesh):
    fine = Mesh(mesh.devices.reshape(4, 2, 4, 8), ("y", "core", "x", "z"))
    clips = P(DP, SEQ, None, None)
    weight = P(SEQ, None)
    return jax.shard_map(
        per_device,
        mesh=fine,
        in_specs=(clips, clips, clips, clips, weight, weight),
        out_specs=(P(DP), clips, clips, weight, weight),
        check_vma=False,
    )
```

```python
import functools

import jax
import jax.numpy as jnp
from jax import lax
from jax.experimental import pallas as pl
from jax.experimental.pallas import tpu as pltpu
from jax.sharding import Mesh, PartitionSpec as P

HEADS = 16
D = 1152
E = D // HEADS
TOKENS = 128
LANES = 128
SEQ = ("x", "z")
DP = ("y", "core")
HUBER_DELTA = 0.03
CELLS = 64 * 64 * D
SCALING = E ** (-0.5)
BF16 = jnp.bfloat16
F32 = jnp.float32
VMEM_BYTES = 63 * 1024 * 1024

NN = (((1,), (0,)), ((), ()))
NT = (((1,), (1,)), ((), ()))
TN = (((0,), (0,)), ((), ()))


def mul(left, right, dims):
    return lax.dot_general(left, right, dims, preferred_element_type=F32)


def window(head):
    low = E * head // LANES
    high = (E * head + E - 1) // LANES + 1
    return low * LANES, high * LANES


def head_mask(head, low, high):
    lane = lax.broadcasted_iota(jnp.int32, (TOKENS, high - low), 1) + low
    return jnp.where((lane >= E * head) & (lane < E * head + E), 1.0, 0.0).astype(BF16)


def same_sequence(temporal):
    row = lax.broadcasted_iota(jnp.int32, (TOKENS, TOKENS), 0)
    col = lax.broadcasted_iota(jnp.int32, (TOKENS, TOKENS), 1)
    if temporal:
        return (row & 1) == (col & 1)
    return (row >> 6) == (col >> 6)


def natural_from_sent():
    nat = lax.broadcasted_iota(jnp.int32, (TOKENS, TOKENS), 0)
    sent = lax.broadcasted_iota(jnp.int32, (TOKENS, TOKENS), 1)
    goes = ((sent >> 1) & 1) * 64 + (sent >> 2) * 2 + (sent & 1)
    return jnp.where(nat == goes, 1.0, 0.0).astype(BF16)


class Tiles:
    def __init__(self, ref, offset, scale=None):
        self.ref, self.offset, self.scale, self.pending = ref, offset, scale, None

    def add(self, head, value):
        low, high = window(head)
        for tile in range(low, high, LANES):
            part = value[:, tile - low : tile - low + LANES]
            if E * head > tile:
                part = self.pending + part
            if E * head + E >= tile + LANES:
                if self.scale is not None:
                    part = part * self.scale
                at = self.offset + tile
                self.ref[:, at : at + LANES] = part.astype(self.ref.dtype)
            else:
                self.pending = part


def attend_heads(temporal, x_ref, mix_ref, probs_ref):
    same = same_sequence(temporal)
    out = Tiles(mix_ref, 0)
    for head in range(HEADS):
        low, high = window(head)
        mask = head_mask(head, low, high)
        queries = x_ref[:, low:high]
        keys = x_ref[:, D + low : D + high] * mask
        values = x_ref[:, 2 * D + low : 2 * D + high] * mask
        scores = jnp.where(same, mul(queries, keys, NT) * SCALING, -1e30)
        powers = jnp.exp(scores - jnp.max(scores, axis=1, keepdims=True))
        probs = powers / jnp.sum(powers, axis=1, keepdims=True)
        probs_ref[head] = probs
        out.add(head, mul(probs.astype(BF16), values, NN))


def attend_space_kernel(place_ref, x_ref, mix_ref, probs_ref, order_ref, mix):
    at_x, at_y, at_z = place_ref[0], place_ref[2], place_ref[3]
    column = lax.broadcasted_iota(jnp.int32, (D, LANES), 0)
    for tile in range(0, D, LANES):
        lane = lax.broadcasted_iota(jnp.int32, (1, LANES), 1) + tile
        block = (lane * 1821) >> 16
        from_z = (at_z + 2 * (((block >> 1) + at_y) & 3) + (block & 1)) & 7
        from_x = ((block >> 3) + at_x) & 3
        source = (from_x * 8 + from_z) * 36 + (lane - block * 36)
        order_ref[:, tile : tile + LANES] = jnp.where(column == source, 1.0, 0.0).astype(BF16)
    attend_heads(False, x_ref, mix, probs_ref)
    mix_ref[...] = mul(mix[...], order_ref[...], NN).astype(BF16)


ROWS = jax.ShapeDtypeStruct((TOKENS, D), BF16)
PROBS = jax.ShapeDtypeStruct((HEADS, TOKENS, TOKENS), F32)


def sent_rows(width):
    return jax.ShapeDtypeStruct((32, 4, width), BF16)


def specs(**places):
    kinds = {"smem": pltpu.SMEM, "vmem": pltpu.VMEM, "any": pl.ANY}
    return [pl.BlockSpec(memory_space=kinds[k]) for k, n in places.items() for _ in range(n)]


def call(kernel, out_shape, in_specs, scratch, name, micros=3, out_specs=None):
    return pl.pallas_call(
        kernel,
        out_shape=out_shape,
        in_specs=in_specs,
        **({} if out_specs is None else {"out_specs": out_specs}),
        scratch_shapes=scratch,
        cost_estimate=pl.CostEstimate(flops=micros * 10**9, bytes_accessed=1, transcendentals=0),
        compiler_params=pltpu.CompilerParams(vmem_limit_bytes=VMEM_BYTES),
        name=name,
    )


def attend_space(place, x):
    order = jax.ShapeDtypeStruct((D, D), BF16)
    return call(
        attend_space_kernel,
        (ROWS, PROBS, order),
        specs(smem=1, vmem=1),
        [pltpu.VMEM((TOKENS, D), BF16)],
        "attend_space",
    )(place, x)


def attend_time_kernel(x_ref, mix_ref, probs_ref, x, mix):
    x[...] = x_ref[...].reshape(TOKENS, 3 * D)
    attend_heads(True, x, mix, probs_ref)
    mix_ref[...] = mix[...].reshape(32, 4, D)


def attend_time(x):
    scratch = [pltpu.VMEM((TOKENS, 3 * D), BF16), pltpu.VMEM((TOKENS, D), BF16)]
    return call(attend_time_kernel, (sent_rows(D), PROBS), specs(vmem=1), scratch, "attend_time")(x)


def send_kernel(x_ref, out_ref):
    out_ref[...] = mul(natural_from_sent(), x_ref[...], TN).astype(BF16).reshape(32, 4, 3 * D)


def send(x):
    return call(send_kernel, sent_rows(3 * D), specs(vmem=1), [], "send_order")(x)


def receive_kernel(x_ref, out_ref):
    x = x_ref[...].reshape(TOKENS, 3 * D)
    out_ref[...] = mul(natural_from_sent(), x, NN).astype(BF16)


def receive(x):
    out = jax.ShapeDtypeStruct((TOKENS, 3 * D), BF16)
    return call(receive_kernel, out, specs(vmem=1), [], "natural_order")(x)


def attend_back_heads(inv, x_ref, probs_ref, grad_ref, out_ref):
    query_out = Tiles(out_ref, 0)
    key_out = Tiles(out_ref, D)
    value_out = Tiles(out_ref, 2 * D, inv)
    for head in range(HEADS):
        low, high = window(head)
        mask = head_mask(head, low, high)
        queries = x_ref[:, low:high] * mask
        keys = x_ref[:, D + low : D + high] * mask
        values = x_ref[:, 2 * D + low : 2 * D + high]
        grads = grad_ref[:, low:high] * mask
        probs = probs_ref[head]
        value_out.add(head, mul(probs.astype(BF16), grads, TN))
        prob_grad = mul(grads, values, NT)
        inner = jnp.sum(prob_grad * probs, axis=1, keepdims=True)
        score_grad = (probs * (prob_grad - inner) * (SCALING * inv)).astype(BF16)
        query_out.add(head, mul(score_grad, keys, NN))
        key_out.add(head, mul(score_grad, queries, TN))


def spread_kernel(grad_ref, spread_ref):
    total = 0.25 * jnp.sum(grad_ref[:, :, D:].reshape(TOKENS, LANES).astype(F32))
    spread_ref[...] = jnp.sqrt(jnp.full((8, LANES), total, F32) / CELLS + HUBER_DELTA**2)


def spread_of(grad):
    out = jax.ShapeDtypeStruct((8, LANES), F32)
    return call(spread_kernel, out, specs(vmem=1), [], "spread", 1)(grad)


def attend_back_time_kernel(x_ref, probs_ref, grad_ref, spread_ref, out_ref, x, grad, out):
    x[...] = x_ref[...].reshape(TOKENS, 3 * D)
    grad[...] = grad_ref[:, :, :D].reshape(TOKENS, D)
    inv = 1.0 / spread_ref[0:1, 0:1]
    attend_back_heads(inv, x, probs_ref, grad, out)
    out_ref[...] = out[...].reshape(32, 4, 3 * D)


def attend_back_time(x, probs, grad, spread):
    wide = pltpu.VMEM((TOKENS, 3 * D), BF16)
    return call(
        attend_back_time_kernel,
        sent_rows(3 * D),
        specs(vmem=4),
        [wide, pltpu.VMEM((TOKENS, D), BF16), wide],
        "attend_back_time",
        5,
    )(x, probs, grad, spread)


def attend_back_space_kernel(x_ref, probs_ref, grad_ref, spread_ref, out_ref):
    attend_back_heads(1.0 / spread_ref[0:1, 0:1], x_ref, probs_ref, grad_ref, out_ref)


def attend_back_space(x, probs, grad, spread):
    return call(
        attend_back_space_kernel,
        jax.ShapeDtypeStruct((TOKENS, 3 * D), BF16),
        specs(vmem=4),
        [],
        "attend_back_space",
        1,
    )(x, probs, grad, spread)


def fetch_weights(refs, weight, sems):
    copies = []
    for a in range(4):
        copy = pltpu.make_async_copy(refs[a], weight.at[pl.ds(288 * a, 288)], sems.at[a])
        copy.start()
        copies.append(copy)
    return copies


def project_kernel(place_ref, time_ref, hidden_any, target_any, space_any, order_any, *rest):
    own_refs, other_refs = rest[0:4], rest[4:8]
    time_grad_ref, space_grad_ref, pack_refs = rest[8], rest[9], rest[10:14]
    weights, hidden_ref, target_ref, space_ref, order_ref, packs, sems = rest[14:]
    at_core = place_ref[1]
    loads = [
        pltpu.make_async_copy(source, place, sems.at[2, n])
        for n, (source, place) in enumerate(
            ((order_any, order_ref), (hidden_any, hidden_ref), (target_any, target_ref), (space_any, space_ref))
        )
    ]
    for copy in loads:
        copy.start()
    copies = fetch_weights(own_refs, weights.at[at_core], sems.at[0])
    copies += fetch_weights(other_refs, weights.at[1 - at_core], sems.at[1])
    natural = natural_from_sent()
    for copy in loads:
        copy.wait()
    time_mix = mul(natural, time_ref[...].reshape(TOKENS, D), NN).astype(BF16)
    time_mix = mul(time_mix, order_ref[...], NN).astype(BF16)
    base = hidden_ref[...].astype(F32) - target_ref[...].astype(F32)
    for copy in copies:
        copy.wait()
    resid = (
        base
        + mul(space_ref[...], weights[0], NN)
        + mul(time_mix, weights[1], NN)
    )
    total = jnp.sum(resid * resid)
    out_grad = resid.astype(BF16)
    time_grad = mul(out_grad, weights[1], NT).astype(BF16)
    time_grad = mul(time_grad, order_ref[...], NT).astype(BF16)
    time_grad = mul(natural, time_grad, TN).astype(BF16)
    lane = lax.broadcasted_iota(jnp.int32, (TOKENS, LANES), 1)
    whole = jnp.full((TOKENS, LANES), total, F32)
    first = whole.astype(BF16).astype(F32)
    second = (whole - first).astype(BF16).astype(F32)
    third = whole - first - second
    parts = jnp.where(lane == 0, first, jnp.where(lane == 1, second, jnp.where(lane == 2, third, 0.0)))
    time_grad_ref[:, :, :D] = time_grad.reshape(32, 4, D)
    time_grad_ref[:, :, D:] = parts.astype(BF16).reshape(32, 4, LANES)
    stores = []
    for a in range(4):
        packs[a, :, :D] = out_grad
        packs[a, :, D:] = jnp.concatenate(
            [space_ref[:, 288 * a : 288 * a + 288], time_mix[:, 288 * a : 288 * a + 288]], axis=1
        )
        stores.append(pltpu.make_async_copy(packs.at[a], pack_refs[a], sems.at[3, a]))
        stores[-1].start()
    space_grad = mul(out_grad, weights[0], NT).astype(BF16)
    space_grad_ref[...] = mul(space_grad, order_ref[...], NT).astype(BF16)
    for copy in stores:
        copy.wait()


def project(place, hidden, target, space_mix, time_mix, order, own, other):
    packed = jax.ShapeDtypeStruct((TOKENS, D + 576), BF16)
    return call(
        project_kernel,
        (sent_rows(D + LANES), ROWS) + (packed,) * 4,
        specs(smem=1, vmem=1, any=12),
        [pltpu.VMEM((2, D, D), BF16)]
        + [pltpu.VMEM((TOKENS, D), BF16)] * 3
        + [
            pltpu.VMEM((D, D), BF16),
            pltpu.VMEM((4, TOKENS, D + 576), BF16),
            pltpu.SemaphoreType.DMA((4, 4)),
        ],
        "project",
        8,
        specs(vmem=2, any=4),
    )(place, time_mix, hidden, target, space_mix, order, *own, *other)


def weight_kernel(place_ref, *rest):
    spread_refs, pack_refs = rest[0:2], rest[2:10]
    out_ref, total = rest[10:]
    first = place_ref[1] == 0
    for n, pack_ref in enumerate(pack_refs):
        inv = 1.0 / spread_refs[n // 4][0:1, 0:1]
        out_grad = (pack_ref[:, :D].astype(F32) * inv).astype(BF16)
        mix = jnp.where(first, pack_ref[:, D : D + 288], pack_ref[:, D + 288 :])
        term = mul(mix, out_grad, TN)
        if n == 0:
            total[...] = term
        else:
            total[...] += term
    out_ref[...] = total[...].astype(BF16)


def weight_grad(place, spreads, packs):
    return call(
        weight_kernel,
        jax.ShapeDtypeStruct((288, D), BF16),
        specs(smem=1, vmem=10),
        [pltpu.VMEM((288, D), F32)],
        "weight_grad",
    )(place, *spreads, *packs)


def finish_kernel(place_ref, own_ref, other_ref, space_ref, time_ref):
    own, other = own_ref[...].astype(F32), other_ref[...].astype(F32)
    first = place_ref[1] == 0
    space_ref[...] = jnp.where(first, own, other)
    time_ref[...] = jnp.where(first, other, own)


def finish(place, own, other):
    rows = jax.ShapeDtypeStruct((36, D), F32)
    return call(finish_kernel, (rows, rows), specs(smem=1, vmem=2), [], "finish")(place, own, other)


def shift_z(value, slope, extra):
    extra = extra if slope > 0 else -extra
    pairs = [(8 * y + z, 8 * y + (z + slope * y + extra) % 8) for y in range(4) for z in range(8)]
    return lax.ppermute(value, ("y", "z"), pairs)


def shift(value, axis, size, step):
    return lax.ppermute(value, axis, [(i, (i + step) % size) for i in range(size)])


def swap(value):
    return lax.ppermute(value, "core", [(0, 1), (1, 0)])


def after(*values):
    return lax.optimization_barrier(values)


def add(blocks):
    return sum(block.astype(F32) for block in blocks).astype(BF16)


def exchange(value, axis):
    return lax.all_to_all(value, axis, split_axis=0, concat_axis=0, tiled=True)


def per_device(hidden_in, spatial_qkv, temporal_qkv, teacher_target, spatial_proj, temporal_proj):
    at_x, at_core, at_y, at_z = (lax.axis_index(a) for a in ("x", "core", "y", "z"))
    place = jnp.stack([at_x, at_core, at_y, at_z]).astype(jnp.int32)

    rows = jnp.where(at_core == 0, spatial_proj, temporal_proj)
    by_z = jnp.concatenate([shift_z(rows, -2, 0), shift_z(rows, -2, 1)])
    by_z, temporal_qkv = after(by_z, temporal_qkv)
    time_x = exchange(send(temporal_qkv.reshape(TOKENS, 3 * D)), SEQ)
    by_y = jnp.concatenate([by_z] + [shift(by_z, "y", 4, 4 - a) for a in range(1, 4)])

    by_y, spatial_qkv = after(by_y, spatial_qkv)
    space_x = spatial_qkv.reshape(TOKENS, 3 * D)
    space_mix, space_probs, order = attend_space(place, space_x)
    time_x, space_mix, space_probs, order = after(time_x, space_mix, space_probs, order)
    time_mix, time_probs = attend_time(time_x)
    time_mix = exchange(time_mix, SEQ)
    own = [by_y] + [shift(by_y, "x", 4, 4 - b) for b in range(1, 4)]
    other = [swap(own[0])]
    time_mix, own[1], own[2], own[3] = after(time_mix, own[1], own[2], own[3])
    other += [swap(block) for block in own[1:]]

    time_grad, space_grad, *packs = project(
        place,
        hidden_in.reshape(TOKENS, D),
        teacher_target.reshape(TOKENS, D),
        space_mix,
        time_mix,
        order,
        own,
        other,
    )
    time_back = exchange(time_grad, SEQ)
    packs = [packs[0]] + [shift(packs[b], "x", 4, b) for b in range(1, 4)]
    spread = spread_of(time_back)
    clip_loss = spread[0, :1] - HUBER_DELTA
    spreads = [spread, swap(spread)]
    time_out = attend_back_time(time_x, time_probs, time_back, spread)
    time_out, spread, packs = after(time_out, spread, packs)
    time_out = exchange(time_out, SEQ)
    packs = packs + [swap(block) for block in packs]

    spatial_qkv_grad = attend_back_space(space_x, space_probs, space_grad, spread)

    partial = weight_grad(place, spreads, packs)
    partial = add([partial[:72]] + [shift(partial[72 * a : 72 * a + 72], "y", 4, a) for a in range(1, 4)])
    piece = add([shift_z(partial[:36], 2, 0), shift_z(partial[36:], 2, 1)])
    piece, time_out, spatial_qkv_grad = after(piece, time_out, spatial_qkv_grad)
    ends = [shift(piece, "y", 4, a).astype(F32) for a in range(1, 4)]
    final = ((piece.astype(F32) + ends[1]) + (ends[0] + ends[2])).astype(BF16)
    spatial_proj_grad, temporal_proj_grad = finish(place, final, swap(final))
    temporal_qkv_grad = receive(time_out)
    return (
        clip_loss,
        spatial_qkv_grad.reshape(1, 2, 64, 3 * D),
        temporal_qkv_grad.reshape(1, 2, 64, 3 * D),
        spatial_proj_grad,
        temporal_proj_grad,
    )


def solution(mesh):
    fine = Mesh(mesh.devices.reshape(4, 2, 4, 8), ("y", "core", "x", "z"))
    clips = P(DP, SEQ, None, None)
    weight = P(SEQ, None)
    return jax.shard_map(
        per_device,
        mesh=fine,
        in_specs=(clips, clips, clips, clips, weight, weight),
        out_specs=(P(DP), clips, clips, weight, weight),
        check_vma=False,
    )
```

```python
import functools

import jax
import jax.numpy as jnp
from jax import lax
from jax.experimental import pallas as pl
from jax.experimental.pallas import tpu as pltpu
from jax.sharding import Mesh, PartitionSpec as P

HEADS = 16

D = 1152
E = D // HEADS
TOKENS = 128
LANES = 128
SEQ = ("x", "z")
DP = ("y", "core")
HUBER_DELTA = 0.03
CELLS = 64 * 64 * D
SCALING = E ** (-0.5)
BF16 = jnp.bfloat16
F32 = jnp.float32
VMEM_BYTES = 63 * 1024 * 1024

NN = (((1,), (0,)), ((), ()))
NT = (((1,), (1,)), ((), ()))
TN = (((0,), (0,)), ((), ()))

def mul(left, right, dims):
    return lax.dot_general(left, right, dims, preferred_element_type=F32)

def window(head):
    low = E * head // LANES
    high = (E * head + E - 1) // LANES + 1
    return low * LANES, high * LANES

def head_mask(head, low, high):
    lane = lax.broadcasted_iota(jnp.int32, (TOKENS, high - low), 1) + low
    return jnp.where((lane >= E * head) & (lane < E * head + E), 1.0, 0.0).astype(BF16)

def same_sequence(temporal):
    row = lax.broadcasted_iota(jnp.int32, (TOKENS, TOKENS), 0)
    col = lax.broadcasted_iota(jnp.int32, (TOKENS, TOKENS), 1)
    if temporal:
        return (row & 1) == (col & 1)
    return (row >> 6) == (col >> 6)

def natural_from_sent():
    nat = lax.broadcasted_iota(jnp.int32, (TOKENS, TOKENS), 0)
    sent = lax.broadcasted_iota(jnp.int32, (TOKENS, TOKENS), 1)
    goes = ((sent >> 1) & 1) * 64 + (sent >> 2) * 2 + (sent & 1)
    return jnp.where(nat == goes, 1.0, 0.0).astype(BF16)

class Tiles:
    def __init__(self, ref, offset, scale=None):
        self.ref, self.offset, self.scale, self.pending = ref, offset, scale, None

    def add(self, head, value):
        low, high = window(head)
        for tile in range(low, high, LANES):
            part = value[:, tile - low : tile - low + LANES]
            if E * head > tile:
                part = self.pending + part
            if E * head + E >= tile + LANES:
                if self.scale is not None:
                    part = part * self.scale
                at = self.offset + tile
                self.ref[:, at : at + LANES] = part.astype(self.ref.dtype)
            else:
                self.pending = part

def attend_heads(temporal, x_ref, mix_ref, probs_ref):
    same = same_sequence(temporal)
    out = Tiles(mix_ref, 0)
    for head in range(HEADS):
        low, high = window(head)
        mask = head_mask(head, low, high)
        queries = x_ref[:, low:high]
        keys = x_ref[:, D + low : D + high] * mask
        values = x_ref[:, 2 * D + low : 2 * D + high] * mask
        scores = jnp.where(same, mul(queries, keys, NT) * SCALING, -1e30)
        powers = jnp.exp(scores - jnp.max(scores, axis=1, keepdims=True))
        probs = powers / jnp.sum(powers, axis=1, keepdims=True)
        probs_ref[head] = probs
        out.add(head, mul(probs.astype(BF16), values, NN))

def attend_space_kernel(place_ref, x_ref, mix_ref, probs_ref, order_ref, mix):
    at_x, at_y, at_z = place_ref[0], place_ref[2], place_ref[3]
    column = lax.broadcasted_iota(jnp.int32, (D, LANES), 0)
    for tile in range(0, D, LANES):
        lane = lax.broadcasted_iota(jnp.int32, (1, LANES), 1) + tile
        block = (lane * 1821) >> 16
        from_z = (at_z + (((block >> 1) + at_y) & 3) + 4 * (block & 1)) & 7
        from_x = ((block >> 3) + at_x) & 3
        source = (from_x * 8 + from_z) * 36 + (lane - block * 36)
        order_ref[:, tile : tile + LANES] = jnp.where(column == source, 1.0, 0.0).astype(BF16)
    attend_heads(False, x_ref, mix, probs_ref)
    mix_ref[...] = mul(mix[...], order_ref[...], NN).astype(BF16)

ROWS = jax.ShapeDtypeStruct((TOKENS, D), BF16)
PROBS = jax.ShapeDtypeStruct((HEADS, TOKENS, TOKENS), F32)

def sent_rows(width):
    return jax.ShapeDtypeStruct((32, 4, width), BF16)

def specs(**places):
    kinds = {"smem": pltpu.SMEM, "vmem": pltpu.VMEM, "any": pl.ANY}
    return [pl.BlockSpec(memory_space=kinds[k]) for k, n in places.items() for _ in range(n)]

def call(kernel, out_shape, in_specs, scratch, name, micros=3, out_specs=None):
    return pl.pallas_call(
        kernel,
        out_shape=out_shape,
        in_specs=in_specs,
        **({} if out_specs is None else {"out_specs": out_specs}),
        scratch_shapes=scratch,
        cost_estimate=pl.CostEstimate(flops=micros * 10**9, bytes_accessed=1, transcendentals=0),
        compiler_params=pltpu.CompilerParams(vmem_limit_bytes=VMEM_BYTES),
        name=name,
    )

def attend_space(place, x):
    order = jax.ShapeDtypeStruct((D, D), BF16)
    return call(
        attend_space_kernel,
        (ROWS, PROBS, order),
        specs(smem=1, vmem=1),
        [pltpu.VMEM((TOKENS, D), BF16)],
        "attend_space",
        14,
    )(place, x)

def stack_kernel(*refs):
    *block_refs, out_ref = refs
    for a, ref in enumerate(block_refs):
        out_ref[72 * a : 72 * a + 72] = ref[...]

def stack(blocks):
    out = jax.ShapeDtypeStruct((288, D), BF16)
    return call(stack_kernel, out, specs(vmem=4), [], "stack", 1)(*blocks)

def attend_time_kernel(x_ref, mix_ref, probs_ref, x, mix):
    x[...] = x_ref[...].reshape(TOKENS, 3 * D)
    attend_heads(True, x, mix, probs_ref)
    mix_ref[...] = mix[...].reshape(32, 4, D)

def attend_time(x):
    scratch = [pltpu.VMEM((TOKENS, 3 * D), BF16), pltpu.VMEM((TOKENS, D), BF16)]
    return call(attend_time_kernel, (sent_rows(D), PROBS), specs(vmem=1), scratch, "attend_time")(x)

def send_kernel(x_ref, out_ref):
    out_ref[...] = mul(natural_from_sent(), x_ref[...], TN).astype(BF16).reshape(32, 4, 3 * D)

def send(x):
    return call(send_kernel, sent_rows(3 * D), specs(vmem=1), [], "send_order")(x)

def receive_kernel(x_ref, out_ref):
    x = x_ref[...].reshape(TOKENS, 3 * D)
    out_ref[...] = mul(natural_from_sent(), x, NN).astype(BF16)

def receive(x):
    out = jax.ShapeDtypeStruct((TOKENS, 3 * D), BF16)
    return call(receive_kernel, out, specs(vmem=1), [], "natural_order")(x)

def attend_back_heads(inv, x_ref, probs_ref, grad_ref, out_ref):
    query_out = Tiles(out_ref, 0)
    key_out = Tiles(out_ref, D)
    value_out = Tiles(out_ref, 2 * D, inv)
    for head in range(HEADS):
        low, high = window(head)
        mask = head_mask(head, low, high)
        queries = x_ref[:, low:high] * mask
        keys = x_ref[:, D + low : D + high] * mask
        values = x_ref[:, 2 * D + low : 2 * D + high]
        grads = grad_ref[:, low:high] * mask
        probs = probs_ref[head]
        value_out.add(head, mul(probs.astype(BF16), grads, TN))
        prob_grad = mul(grads, values, NT)
        inner = jnp.sum(prob_grad * probs, axis=1, keepdims=True)
        score_grad = (probs * (prob_grad - inner) * (SCALING * inv)).astype(BF16)
        query_out.add(head, mul(score_grad, keys, NN))
        key_out.add(head, mul(score_grad, queries, TN))

def attend_back_time_kernel(x_ref, probs_ref, grad_ref, out_ref, spread_ref, x, grad, out):
    x[...] = x_ref[...].reshape(TOKENS, 3 * D)
    grad[...] = grad_ref[:, :, :D].reshape(TOKENS, D)
    total = 0.25 * jnp.sum(grad_ref[:, :, D:].reshape(TOKENS, LANES).astype(F32))
    spread = jnp.sqrt(jnp.full((8, LANES), total, F32) / CELLS + HUBER_DELTA**2)
    spread_ref[...] = spread
    inv = 1.0 / spread[0:1, 0:1]
    attend_back_heads(inv, x, probs_ref, grad, out)
    out_ref[...] = out[...].reshape(32, 4, 3 * D)

def attend_back_time(x, probs, grad):
    wide = pltpu.VMEM((TOKENS, 3 * D), BF16)
    return call(
        attend_back_time_kernel,
        (sent_rows(3 * D), jax.ShapeDtypeStruct((8, LANES), F32)),
        specs(vmem=3),
        [wide, pltpu.VMEM((TOKENS, D), BF16), wide],
        "attend_back_time",
        5,
    )(x, probs, grad)

def attend_back_space_kernel(x_ref, probs_ref, grad_ref, spread_ref, out_ref):
    attend_back_heads(1.0 / spread_ref[0:1, 0:1], x_ref, probs_ref, grad_ref, out_ref)

def attend_back_space(x, probs, grad, spread):
    return call(
        attend_back_space_kernel,
        jax.ShapeDtypeStruct((TOKENS, 3 * D), BF16),
        specs(vmem=4),
        [],
        "attend_back_space",
        1,
    )(x, probs, grad, spread)

def fetch_weights(refs, weight, sems):
    copies = []
    for a in range(4):
        copy = pltpu.make_async_copy(refs[a], weight.at[pl.ds(288 * a, 288)], sems.at[a])
        copy.start()
        copies.append(copy)
    return copies

def project_kernel(place_ref, time_ref, hidden_any, target_any, space_any, order_any, *rest):
    own_refs, other_refs = rest[0:4], rest[4:8]
    time_grad_ref, pack_refs = rest[8], rest[9:13]
    weights, hidden_ref, target_ref, space_ref, order_ref, packs, sems = rest[13:]
    at_core = place_ref[1]
    loads = [
        pltpu.make_async_copy(source, place, sems.at[2, n])
        for n, (source, place) in enumerate(
            ((order_any, order_ref), (hidden_any, hidden_ref), (target_any, target_ref), (space_any, space_ref))
        )
    ]
    for copy in loads:
        copy.start()
    copies = fetch_weights(own_refs, weights.at[at_core], sems.at[0])
    copies += fetch_weights(other_refs, weights.at[1 - at_core], sems.at[1])
    natural = natural_from_sent()
    for copy in loads:
        copy.wait()
    time_mix = mul(natural, time_ref[...].reshape(TOKENS, D), NN).astype(BF16)
    time_mix = mul(time_mix, order_ref[...], NN).astype(BF16)
    base = hidden_ref[...].astype(F32) - target_ref[...].astype(F32)
    first = at_core == 0
    space_mix = space_ref[...]
    for copy in copies[:4]:
        copy.wait()
    resid = base + mul(jnp.where(first, space_mix, time_mix), weights[at_core], NN)
    for copy in copies[4:]:
        copy.wait()
    resid = resid + mul(jnp.where(first, time_mix, space_mix), weights[1 - at_core], NN)
    total = jnp.sum(resid * resid)
    out_grad = resid.astype(BF16)
    time_grad = mul(out_grad, weights[1], NT).astype(BF16)
    time_grad = mul(time_grad, order_ref[...], NT).astype(BF16)
    time_grad = mul(natural, time_grad, TN).astype(BF16)
    lane = lax.broadcasted_iota(jnp.int32, (TOKENS, LANES), 1)
    whole = jnp.full((TOKENS, LANES), total, F32)
    first = whole.astype(BF16).astype(F32)
    second = (whole - first).astype(BF16).astype(F32)
    third = whole - first - second
    parts = jnp.where(lane == 0, first, jnp.where(lane == 1, second, jnp.where(lane == 2, third, 0.0)))
    time_grad_ref[:, :, :D] = time_grad.reshape(32, 4, D)
    time_grad_ref[:, :, D:] = parts.astype(BF16).reshape(32, 4, LANES)
    stores = []
    for a in range(4):
        packs[a, :, :D] = out_grad
        packs[a, :, D:] = jnp.concatenate(
            [space_ref[:, 288 * a : 288 * a + 288], time_mix[:, 288 * a : 288 * a + 288]], axis=1
        )
        stores.append(pltpu.make_async_copy(packs.at[a], pack_refs[a], sems.at[3, a]))
        stores[-1].start()
    for copy in stores:
        copy.wait()

def project(place, hidden, target, space_mix, time_mix, order, own, other):
    packed = jax.ShapeDtypeStruct((TOKENS, D + 576), BF16)
    return call(
        project_kernel,
        (sent_rows(D + LANES),) + (packed,) * 4,
        specs(smem=1, vmem=1, any=12),
        [pltpu.VMEM((2, D, D), BF16)]
        + [pltpu.VMEM((TOKENS, D), BF16)] * 3
        + [
            pltpu.VMEM((D, D), BF16),
            pltpu.VMEM((4, TOKENS, D + 576), BF16),
            pltpu.SemaphoreType.DMA((4, 4)),
        ],
        "project",
        8,
        specs(vmem=1, any=4),
    )(place, time_mix, hidden, target, space_mix, order, *own, *other)

def space_back_kernel(place_ref, pack_ref, order_ref, *rest):
    own_refs, other_refs = rest[0:4], rest[4:8]
    out_ref, weight, sems = rest[8:]
    first = place_ref[1] == 0

    @pl.when(first)
    def _():
        for copy in fetch_weights(own_refs, weight, sems):
            copy.wait()

    @pl.when(jnp.logical_not(first))
    def _():
        for copy in fetch_weights(other_refs, weight, sems):
            copy.wait()

    mix_grad = mul(pack_ref[:, :D], weight[...], NT).astype(BF16)
    out_ref[...] = mul(mix_grad, order_ref[...], NT).astype(BF16)

def space_back(place, packed, order, own, other):
    scratch = [pltpu.VMEM((D, D), BF16), pltpu.SemaphoreType.DMA((4,))]
    return call(
        space_back_kernel, ROWS, specs(smem=1, vmem=2, any=8), scratch, "space_back", 3
    )(place, packed, order, *own, *other)

def weight_kernel(place_ref, *rest):
    spread_refs, pack_refs = rest[0:2], rest[2:10]
    out_refs, total = rest[10:14], rest[14]
    first = place_ref[1] == 0
    for n, pack_ref in enumerate(pack_refs):
        inv = 1.0 / spread_refs[n // 4][0:1, 0:1]
        out_grad = (pack_ref[:, :D].astype(F32) * inv).astype(BF16)
        mix = jnp.where(first, pack_ref[:, D : D + 288], pack_ref[:, D + 288 :])
        term = mul(mix, out_grad, TN)
        if n == 0:
            total[...] = term
        else:
            total[...] += term
    for a in range(4):
        out_refs[a][...] = total[72 * a : 72 * a + 72].astype(BF16)

def weight_grad(place, spreads, packs):
    return call(
        weight_kernel,
        (jax.ShapeDtypeStruct((72, D), BF16),) * 4,
        specs(smem=1, vmem=10),
        [pltpu.VMEM((288, D), F32)],
        "weight_grad",
        8,
    )(place, *spreads, *packs)

def halves_kernel(*refs):
    *block_refs, first_ref, second_ref = refs
    total = sum(ref[...].astype(F32) for ref in block_refs)
    first_ref[...] = total[:36].astype(BF16)
    second_ref[...] = total[36:].astype(BF16)

def halves(blocks):
    out = jax.ShapeDtypeStruct((36, D), BF16)
    return call(halves_kernel, (out, out), specs(vmem=4), [], "halves", 0)(*blocks)

def finish_kernel(place_ref, own_ref, other_ref, space_ref, time_ref):
    own, other = own_ref[...].astype(F32), other_ref[...].astype(F32)
    first = place_ref[1] == 0
    space_ref[...] = jnp.where(first, own, other)
    time_ref[...] = jnp.where(first, other, own)

def finish(place, own, other):
    rows = jax.ShapeDtypeStruct((36, D), F32)
    return call(finish_kernel, (rows, rows), specs(smem=1, vmem=2), [], "finish")(place, own, other)

def shift_z(value, slope, extra):
    extra = extra if slope > 0 else -extra
    pairs = [(8 * y + z, 8 * y + (z + slope * y + extra) % 8) for y in range(4) for z in range(8)]
    return lax.ppermute(value, ("y", "z"), pairs)

def shift(value, axis, size, step):
    return lax.ppermute(value, axis, [(i, (i + step) % size) for i in range(size)])

def swap(value):
    return lax.ppermute(value, "core", [(0, 1), (1, 0)])

def after(*values):
    return lax.optimization_barrier(values)

def add(blocks):
    return sum(block.astype(F32) for block in blocks).astype(BF16)

def exchange(value, axis):
    return lax.all_to_all(value, axis, split_axis=0, concat_axis=0, tiled=True)

def per_device(hidden_in, spatial_qkv, temporal_qkv, teacher_target, spatial_proj, temporal_proj):
    at_x, at_core, at_y, at_z = (lax.axis_index(a) for a in ("x", "core", "y", "z"))
    place = jnp.stack([at_x, at_core, at_y, at_z]).astype(jnp.int32)

    rows = jnp.where(at_core == 0, spatial_proj, temporal_proj)
    by_z = jnp.concatenate([shift_z(rows, -1, 0), shift_z(rows, -1, 4)])
    time_x = exchange(send(temporal_qkv.reshape(TOKENS, 3 * D)), SEQ)
    by_y = stack([by_z] + [shift(by_z, "y", 4, 4 - a) for a in range(1, 4)])

    by_y, spatial_qkv = after(by_y, spatial_qkv)
    space_x = spatial_qkv.reshape(TOKENS, 3 * D)
    space_mix, space_probs, order = attend_space(place, space_x)
    time_x, space_mix, space_probs, order = after(time_x, space_mix, space_probs, order)
    time_mix, time_probs = attend_time(time_x)
    time_mix = exchange(time_mix, SEQ)
    own = [by_y] + [shift(by_y, "x", 4, 4 - b) for b in range(1, 4)]
    other = [swap(own[0])]
    time_mix, own[1], own[2], own[3] = after(time_mix, own[1], own[2], own[3])
    other += [swap(block) for block in own[1:]]

    time_grad, *packs = project(
        place,
        hidden_in.reshape(TOKENS, D),
        teacher_target.reshape(TOKENS, D),
        space_mix,
        time_mix,
        order,
        own,
        other,
    )
    time_back = exchange(time_grad, SEQ)
    space_grad = space_back(place, packs[0], order, own, other)
    packs = [packs[0]] + [shift(packs[b], "x", 4, b) for b in range(1, 4)]
    time_back, space_grad = after(time_back, space_grad)
    time_out, spread = attend_back_time(time_x, time_probs, time_back)
    clip_loss = spread[0, :1] - HUBER_DELTA
    _, spread, packs = after(time_out, spread, packs)
    spreads = [spread, swap(spread)]
    time_out = exchange(time_out, SEQ)
    packs = packs + [swap(block) for block in packs]

    spatial_qkv_grad = attend_back_space(space_x, space_probs, space_grad, spread)

    partial = weight_grad(place, spreads, packs)
    partial = halves([partial[0]] + [shift(partial[a], "y", 4, a) for a in range(1, 4)])
    partial, time_out, spatial_qkv_grad = after(partial, time_out, spatial_qkv_grad)
    piece = add([shift_z(partial[0], 1, 0), shift_z(partial[1], 1, 4)])
    ends = [shift(piece, "y", 4, a).astype(F32) for a in range(1, 4)]
    final = ((piece.astype(F32) + ends[1]) + (ends[0] + ends[2])).astype(BF16)
    spatial_proj_grad, temporal_proj_grad = finish(place, final, swap(final))
    temporal_qkv_grad = receive(time_out)
    return (
        clip_loss,
        spatial_qkv_grad.reshape(1, 2, 64, 3 * D),
        temporal_qkv_grad.reshape(1, 2, 64, 3 * D),
        spatial_proj_grad,
        temporal_proj_grad,
    )

def solution(mesh):
    fine = Mesh(mesh.devices.reshape(4, 2, 4, 8), ("y", "core", "x", "z"))
    clips = P(DP, SEQ, None, None)
    weight = P(SEQ, None)
    return jax.shard_map(
        per_device,
        mesh=fine,
        in_specs=(clips, clips, clips, clips, weight, weight),
        out_specs=(P(DP), clips, clips, weight, weight),
        check_vma=False,
    )
```

```python
import functools

import jax
import jax.numpy as jnp
from jax import lax
from jax.experimental import pallas as pl
from jax.experimental.pallas import tpu as pltpu
from jax.sharding import Mesh, PartitionSpec as P

HEADS = 16

D = 1152
E = D // HEADS
TOKENS = 128
LANES = 128
SEQ = ("x", "z")
DP = ("y", "core")
HUBER_DELTA = 0.03
CELLS = 64 * 64 * D
SCALING = E ** (-0.5)
BF16 = jnp.bfloat16
F32 = jnp.float32
VMEM_BYTES = 63 * 1024 * 1024

NN = (((1,), (0,)), ((), ()))
NT = (((1,), (1,)), ((), ()))
TN = (((0,), (0,)), ((), ()))

def mul(left, right, dims):
    return lax.dot_general(left, right, dims, preferred_element_type=F32)

def window(head):
    low = E * head // LANES
    high = (E * head + E - 1) // LANES + 1
    return low * LANES, high * LANES

def head_mask(head, low, high):
    lane = lax.broadcasted_iota(jnp.int32, (TOKENS, high - low), 1) + low
    return jnp.where((lane >= E * head) & (lane < E * head + E), 1.0, 0.0).astype(BF16)

def same_sequence(temporal):
    row = lax.broadcasted_iota(jnp.int32, (TOKENS, TOKENS), 0)
    col = lax.broadcasted_iota(jnp.int32, (TOKENS, TOKENS), 1)
    if temporal:
        return (row & 1) == (col & 1)
    return (row >> 6) == (col >> 6)

def natural_from_sent():
    nat = lax.broadcasted_iota(jnp.int32, (TOKENS, TOKENS), 0)
    sent = lax.broadcasted_iota(jnp.int32, (TOKENS, TOKENS), 1)
    goes = ((sent >> 1) & 1) * 64 + (sent >> 2) * 2 + (sent & 1)
    return jnp.where(nat == goes, 1.0, 0.0).astype(BF16)

class Tiles:
    def __init__(self, ref, offset, scale=None):
        self.ref, self.offset, self.scale, self.pending = ref, offset, scale, None

    def add(self, head, value):
        low, high = window(head)
        for tile in range(low, high, LANES):
            part = value[:, tile - low : tile - low + LANES]
            if E * head > tile:
                part = self.pending + part
            if E * head + E >= tile + LANES:
                if self.scale is not None:
                    part = part * self.scale
                at = self.offset + tile
                self.ref[:, at : at + LANES] = part.astype(self.ref.dtype)
            else:
                self.pending = part

def attend_heads(temporal, x_ref, mix_ref, probs_ref):
    same = same_sequence(temporal)
    out = Tiles(mix_ref, 0)
    for head in range(HEADS):
        low, high = window(head)
        mask = head_mask(head, low, high)
        queries = x_ref[:, low:high]
        keys = x_ref[:, D + low : D + high] * mask
        values = x_ref[:, 2 * D + low : 2 * D + high] * mask
        scores = jnp.where(same, mul(queries, keys, NT) * SCALING, -1e30)
        powers = jnp.exp(scores - jnp.max(scores, axis=1, keepdims=True))
        probs = powers / jnp.sum(powers, axis=1, keepdims=True)
        probs_ref[head] = probs
        out.add(head, mul(probs.astype(BF16), values, NN))

ROWS = jax.ShapeDtypeStruct((TOKENS, D), BF16)
PROBS = jax.ShapeDtypeStruct((HEADS, TOKENS, TOKENS), F32)

def sent_rows(width):
    return jax.ShapeDtypeStruct((32, 4, width), BF16)

def specs(**places):
    kinds = {"smem": pltpu.SMEM, "vmem": pltpu.VMEM, "any": pl.ANY}
    return [pl.BlockSpec(memory_space=kinds[k]) for k, n in places.items() for _ in range(n)]

def call(kernel, out_shape, in_specs, scratch, name, micros=3, out_specs=None, vmem=VMEM_BYTES):
    return pl.pallas_call(
        kernel,
        out_shape=out_shape,
        in_specs=in_specs,
        **({} if out_specs is None else {"out_specs": out_specs}),
        scratch_shapes=scratch,
        cost_estimate=pl.CostEstimate(flops=micros * 10**9, bytes_accessed=1, transcendentals=0),
        compiler_params=pltpu.CompilerParams(vmem_limit_bytes=vmem),
        name=name,
    )

def attend_space(x):
    kernel = functools.partial(attend_heads, False)
    return call(kernel, (ROWS, PROBS), specs(vmem=1), [], "attend_space", 14)(x)


def unit_rows(place_ref):
    at_y, at_z = place_ref[2], place_ref[3]
    natural = lax.broadcasted_iota(jnp.int32, (288, 288), 0)
    unit = lax.broadcasted_iota(jnp.int32, (1, 288), 1)
    block = (unit * 1821) >> 16
    from_z = (at_z + (((block >> 1) + at_y) & 3) + 4 * (block & 1)) & 7
    return jnp.where(natural == from_z * 36 + (unit - block * 36), 1.0, 0.0).astype(BF16)


def stack_kernel(place_ref, *refs):
    *block_refs, out_ref, units = refs
    for a, ref in enumerate(block_refs):
        units[72 * a : 72 * a + 72] = ref[...]
    out_ref[...] = mul(unit_rows(place_ref), units[...], NN).astype(BF16)


def stack(place, blocks):
    out = jax.ShapeDtypeStruct((288, D), BF16)
    scratch = [pltpu.VMEM((288, D), BF16)]
    return call(stack_kernel, out, specs(smem=1, vmem=4), scratch, "stack", 1, vmem=32 * 1024 * 1024)(place, *blocks)


def attend_time_kernel(x_ref, mix_ref, probs_ref, x, mix):
    x[...] = x_ref[...].reshape(TOKENS, 3 * D)
    attend_heads(True, x, mix, probs_ref)
    mix_ref[...] = mix[...].reshape(32, 4, D)

def attend_time(x):
    scratch = [pltpu.VMEM((TOKENS, 3 * D), BF16), pltpu.VMEM((TOKENS, D), BF16)]
    return call(attend_time_kernel, (sent_rows(D), PROBS), specs(vmem=1), scratch, "attend_time")(x)

def send_kernel(x_ref, out_ref):
    out_ref[...] = mul(natural_from_sent(), x_ref[...], TN).astype(BF16).reshape(32, 4, 3 * D)

def send(x):
    return call(send_kernel, sent_rows(3 * D), specs(vmem=1), [], "send_order")(x)

def receive_kernel(x_ref, out_ref):
    x = x_ref[...].reshape(TOKENS, 3 * D)
    out_ref[...] = mul(natural_from_sent(), x, NN).astype(BF16)

def receive(x):
    out = jax.ShapeDtypeStruct((TOKENS, 3 * D), BF16)
    return call(receive_kernel, out, specs(vmem=1), [], "natural_order", vmem=32 * 1024 * 1024)(x)

def attend_back_heads(inv, x_ref, probs_ref, grad_ref, out_ref):
    query_out = Tiles(out_ref, 0)
    key_out = Tiles(out_ref, D)
    value_out = Tiles(out_ref, 2 * D, inv)
    for head in range(HEADS):
        low, high = window(head)
        mask = head_mask(head, low, high)
        queries = x_ref[:, low:high] * mask
        keys = x_ref[:, D + low : D + high] * mask
        values = x_ref[:, 2 * D + low : 2 * D + high]
        grads = grad_ref[:, low:high] * mask
        probs = probs_ref[head]
        value_out.add(head, mul(probs.astype(BF16), grads, TN))
        prob_grad = mul(grads, values, NT)
        inner = jnp.sum(prob_grad * probs, axis=1, keepdims=True)
        score_grad = (probs * (prob_grad - inner) * (SCALING * inv)).astype(BF16)
        query_out.add(head, mul(score_grad, keys, NN))
        key_out.add(head, mul(score_grad, queries, TN))

def attend_back_time_kernel(x_ref, probs_ref, grad_ref, out_ref, spread_ref, x, grad, out):
    x[...] = x_ref[...].reshape(TOKENS, 3 * D)
    grad[...] = grad_ref[:, :, :D].reshape(TOKENS, D)
    total = 0.25 * jnp.sum(grad_ref[:, :, D:].reshape(TOKENS, LANES).astype(F32))
    spread = jnp.sqrt(jnp.full((8, LANES), total, F32) / CELLS + HUBER_DELTA**2)
    spread_ref[...] = spread
    inv = 1.0 / spread[0:1, 0:1]
    attend_back_heads(inv, x, probs_ref, grad, out)
    out_ref[...] = out[...].reshape(32, 4, 3 * D)

def attend_back_time(x, probs, grad):
    wide = pltpu.VMEM((TOKENS, 3 * D), BF16)
    return call(
        attend_back_time_kernel,
        (sent_rows(3 * D), jax.ShapeDtypeStruct((8, LANES), F32)),
        specs(vmem=3),
        [wide, pltpu.VMEM((TOKENS, D), BF16), wide],
        "attend_back_time",
        5,
    )(x, probs, grad)

def attend_back_space_kernel(x_ref, probs_ref, grad_ref, spread_ref, out_ref):
    attend_back_heads(1.0 / spread_ref[0:1, 0:1], x_ref, probs_ref, grad_ref, out_ref)

def attend_back_space(x, probs, grad, spread):
    return call(
        attend_back_space_kernel,
        jax.ShapeDtypeStruct((TOKENS, 3 * D), BF16),
        specs(vmem=4),
        [],
        "attend_back_space",
        1,
        vmem=32 * 1024 * 1024,
    )(x, probs, grad, spread)

def fetch_weights(at_x, refs, weight, sems):
    copies = []
    for b in range(4):
        rows = pl.ds(pl.multiple_of(((at_x + b) & 3) * 288, 288), 288)
        copy = pltpu.make_async_copy(refs[b], weight.at[rows], sems.at[b])
        copy.start()
        copies.append(copy)
    return copies


def column_block(mix, index):
    blocks = [mix[:, 288 * q : 288 * q + 288] for q in range(4)]
    low = jnp.where(index == 0, blocks[0], blocks[1])
    high = jnp.where(index == 2, blocks[2], blocks[3])
    return jnp.where(index < 2, low, high)


def project_kernel(place_ref, time_ref, hidden_any, target_any, space_any, *rest):
    own_refs, other_refs = rest[0:4], rest[4:8]
    time_grad_ref, pack_refs = rest[8], rest[9:13]
    weights, hidden_ref, target_ref, space_ref, packs, sems = rest[13:]
    at_x, at_core = place_ref[0], place_ref[1]
    loads = [
        pltpu.make_async_copy(source, place, sems.at[2, n])
        for n, (source, place) in enumerate(
            ((hidden_any, hidden_ref), (target_any, target_ref), (space_any, space_ref))
        )
    ]
    for copy in loads:
        copy.start()
    copies = fetch_weights(at_x, own_refs, weights.at[at_core], sems.at[0])
    copies += fetch_weights(at_x, other_refs, weights.at[1 - at_core], sems.at[1])
    natural = natural_from_sent()
    for copy in loads:
        copy.wait()
    time_mix = mul(natural, time_ref[...].reshape(TOKENS, D), NN).astype(BF16)
    base = hidden_ref[...].astype(F32) - target_ref[...].astype(F32)
    first = at_core == 0
    space_mix = space_ref[...]
    for copy in copies[:4]:
        copy.wait()
    resid = base + mul(jnp.where(first, space_mix, time_mix), weights[at_core], NN)
    for copy in copies[4:]:
        copy.wait()
    resid = resid + mul(jnp.where(first, time_mix, space_mix), weights[1 - at_core], NN)
    total = jnp.sum(resid * resid)
    out_grad = resid.astype(BF16)
    time_grad = mul(out_grad, weights[1], NT).astype(BF16)
    time_grad = mul(natural, time_grad, TN).astype(BF16)
    lane = lax.broadcasted_iota(jnp.int32, (TOKENS, LANES), 1)
    whole = jnp.full((TOKENS, LANES), total, F32)
    first = whole.astype(BF16).astype(F32)
    second = (whole - first).astype(BF16).astype(F32)
    third = whole - first - second
    parts = jnp.where(lane == 0, first, jnp.where(lane == 1, second, jnp.where(lane == 2, third, 0.0)))
    time_grad_ref[:, :, :D] = time_grad.reshape(32, 4, D)
    time_grad_ref[:, :, D:] = parts.astype(BF16).reshape(32, 4, LANES)
    stores = []
    for a in range(4):
        packs[a, :, :D] = out_grad
        index = (at_x + a) & 3
        packs[a, :, D:] = jnp.concatenate(
            [column_block(space_mix, index), column_block(time_mix, index)], axis=1
        )
        stores.append(pltpu.make_async_copy(packs.at[a], pack_refs[a], sems.at[3, a]))
        stores[-1].start()
    for copy in stores:
        copy.wait()

def project(place, hidden, target, space_mix, time_mix, own, other):
    packed = jax.ShapeDtypeStruct((TOKENS, D + 576), BF16)
    return call(
        project_kernel,
        (sent_rows(D + LANES),) + (packed,) * 4,
        specs(smem=1, vmem=1, any=11),
        [pltpu.VMEM((2, D, D), BF16)]
        + [pltpu.VMEM((TOKENS, D), BF16)] * 3
        + [
            pltpu.VMEM((4, TOKENS, D + 576), BF16),
            pltpu.SemaphoreType.DMA((4, 4)),
        ],
        "project",
        8,
        specs(vmem=1, any=4),
    )(place, time_mix, hidden, target, space_mix, *own, *other)

def space_back_kernel(place_ref, pack_ref, *rest):
    own_refs, other_refs = rest[0:4], rest[4:8]
    out_ref, weight, sems = rest[8:]
    first = place_ref[1] == 0

    @pl.when(first)
    def _():
        for copy in fetch_weights(place_ref[0], own_refs, weight, sems):
            copy.wait()

    @pl.when(jnp.logical_not(first))
    def _():
        for copy in fetch_weights(place_ref[0], other_refs, weight, sems):
            copy.wait()

    out_ref[...] = mul(pack_ref[:, :D], weight[...], NT).astype(BF16)

def space_back(place, packed, own, other):
    scratch = [pltpu.VMEM((D, D), BF16), pltpu.SemaphoreType.DMA((4,))]
    return call(
        space_back_kernel, ROWS, specs(smem=1, vmem=1, any=8), scratch, "space_back", 3
    )(place, packed, *own, *other)

def weight_kernel(place_ref, *rest):
    spread_refs, pack_refs = rest[0:2], rest[2:10]
    out_refs, total = rest[10:14], rest[14]
    first = place_ref[1] == 0
    for n, pack_ref in enumerate(pack_refs):
        inv = 1.0 / spread_refs[n // 4][0:1, 0:1]
        out_grad = (pack_ref[:, :D].astype(F32) * inv).astype(BF16)
        mix = jnp.where(first, pack_ref[:, D : D + 288], pack_ref[:, D + 288 :])
        term = mul(mix, out_grad, TN)
        if n == 0:
            total[...] = term
        else:
            total[...] += term
    units = mul(unit_rows(place_ref), total[...].astype(BF16), TN).astype(BF16)
    for a in range(4):
        out_refs[a][...] = units[72 * a : 72 * a + 72]

def weight_grad(place, spreads, packs):
    return call(
        weight_kernel,
        (jax.ShapeDtypeStruct((72, D), BF16),) * 4,
        specs(smem=1, vmem=10),
        [pltpu.VMEM((288, D), F32)],
        "weight_grad",
        8,
        vmem=32 * 1024 * 1024,
    )(place, *spreads, *packs)

def halves_kernel(*refs):
    *block_refs, first_ref, second_ref = refs
    total = sum(ref[...].astype(F32) for ref in block_refs)
    first_ref[...] = total[:36].astype(BF16)
    second_ref[...] = total[36:].astype(BF16)

def halves(blocks):
    out = jax.ShapeDtypeStruct((36, D), BF16)
    return call(halves_kernel, (out, out), specs(vmem=4), [], "halves", 0, vmem=32 * 1024 * 1024)(*blocks)

def finish_kernel(place_ref, own_ref, other_ref, space_ref, time_ref):
    own, other = own_ref[...].astype(F32), other_ref[...].astype(F32)
    first = place_ref[1] == 0
    space_ref[...] = jnp.where(first, own, other)
    time_ref[...] = jnp.where(first, other, own)

def finish(place, own, other):
    rows = jax.ShapeDtypeStruct((36, D), F32)
    return call(finish_kernel, (rows, rows), specs(smem=1, vmem=2), [], "finish", vmem=32 * 1024 * 1024)(place, own, other)

def shift_z(value, slope, extra):
    extra = extra if slope > 0 else -extra
    pairs = [(8 * y + z, 8 * y + (z + slope * y + extra) % 8) for y in range(4) for z in range(8)]
    return lax.ppermute(value, ("y", "z"), pairs)

def shift(value, axis, size, step):
    return lax.ppermute(value, axis, [(i, (i + step) % size) for i in range(size)])

def swap(value):
    return lax.ppermute(value, "core", [(0, 1), (1, 0)])

def after(*values):
    return lax.optimization_barrier(values)

def add(blocks):
    return sum(block.astype(F32) for block in blocks).astype(BF16)

def exchange(value, axis):
    return lax.all_to_all(value, axis, split_axis=0, concat_axis=0, tiled=True)

def per_device(hidden_in, spatial_qkv, temporal_qkv, teacher_target, spatial_proj, temporal_proj):
    at_x, at_core, at_y, at_z = (lax.axis_index(a) for a in ("x", "core", "y", "z"))
    place = jnp.stack([at_x, at_core, at_y, at_z]).astype(jnp.int32)

    rows = jnp.where(at_core == 0, spatial_proj, temporal_proj)
    by_z = jnp.concatenate([shift_z(rows, -1, 0), shift_z(rows, -1, 4)])
    time_x = exchange(send(temporal_qkv.reshape(TOKENS, 3 * D)), SEQ)
    by_y = stack(place, [by_z] + [shift(by_z, "y", 4, 4 - a) for a in range(1, 4)])

    by_y, spatial_qkv = after(by_y, spatial_qkv)
    space_x = spatial_qkv.reshape(TOKENS, 3 * D)
    space_mix, space_probs = attend_space(space_x)
    time_x, space_mix, space_probs = after(time_x, space_mix, space_probs)
    time_mix, time_probs = attend_time(time_x)
    time_mix = exchange(time_mix, SEQ)
    own = [by_y] + [shift(by_y, "x", 4, 4 - b) for b in range(1, 4)]
    other = [swap(own[0])]
    time_mix, own[1], own[2], own[3] = after(time_mix, own[1], own[2], own[3])
    other += [swap(block) for block in own[1:]]

    time_grad, *packs = project(
        place,
        hidden_in.reshape(TOKENS, D),
        teacher_target.reshape(TOKENS, D),
        space_mix,
        time_mix,
        own,
        other,
    )
    time_back = exchange(time_grad, SEQ)
    space_grad = space_back(place, packs[0], own, other)
    packs = [packs[0]] + [shift(packs[b], "x", 4, b) for b in range(1, 4)]
    time_back, space_grad = after(time_back, space_grad)
    time_out, spread = attend_back_time(time_x, time_probs, time_back)
    clip_loss = spread[0, :1] - HUBER_DELTA
    _, spread, packs = after(time_out, spread, packs)
    spreads = [spread, swap(spread)]
    time_out = exchange(time_out, SEQ)
    packs = packs + [swap(block) for block in packs]

    spatial_qkv_grad = attend_back_space(space_x, space_probs, space_grad, spread)

    partial = weight_grad(place, spreads, packs)
    partial = halves([partial[0]] + [shift(partial[a], "y", 4, a) for a in range(1, 4)])
    partial, time_out, spatial_qkv_grad = after(partial, time_out, spatial_qkv_grad)
    piece = add([shift_z(partial[0], 1, 0), shift_z(partial[1], 1, 4)])
    ends = [shift(piece, "y", 4, a).astype(F32) for a in range(1, 4)]
    final = ((piece.astype(F32) + ends[1]) + (ends[0] + ends[2])).astype(BF16)
    spatial_proj_grad, temporal_proj_grad = finish(place, final, swap(final))
    temporal_qkv_grad = receive(time_out)
    return (
        clip_loss,
        spatial_qkv_grad.reshape(1, 2, 64, 3 * D),
        temporal_qkv_grad.reshape(1, 2, 64, 3 * D),
        spatial_proj_grad,
        temporal_proj_grad,
    )

def solution(mesh):
    fine = Mesh(mesh.devices.reshape(4, 2, 4, 8), ("y", "core", "x", "z"))
    clips = P(DP, SEQ, None, None)
    weight = P(SEQ, None)
    return jax.shard_map(
        per_device,
        mesh=fine,
        in_specs=(clips, clips, clips, clips, weight, weight),
        out_specs=(P(DP), clips, clips, weight, weight),
        check_vma=False,
    )
```

```python
import functools

import jax
import jax.numpy as jnp
from jax import lax
from jax.experimental import pallas as pl
from jax.experimental.pallas import tpu as pltpu
from jax.sharding import Mesh, PartitionSpec as P

HEADS = 16

D = 1152
E = D // HEADS
TOKENS = 128
LANES = 128
SEQ = ("x", "z")
DP = ("y", "core")
HUBER_DELTA = 0.03
CELLS = 64 * 64 * D
SCALING = E ** (-0.5)
BF16 = jnp.bfloat16
F32 = jnp.float32
VMEM_BYTES = 63 * 1024 * 1024

NN = (((1,), (0,)), ((), ()))
NT = (((1,), (1,)), ((), ()))
TN = (((0,), (0,)), ((), ()))

def mul(left, right, dims):
    return lax.dot_general(left, right, dims, preferred_element_type=F32)

def window(head):
    low = E * head // LANES
    high = (E * head + E - 1) // LANES + 1
    return low * LANES, high * LANES

def head_mask(head, low, high):
    lane = lax.broadcasted_iota(jnp.int32, (TOKENS, high - low), 1) + low
    return jnp.where((lane >= E * head) & (lane < E * head + E), 1.0, 0.0).astype(BF16)

def same_sequence(temporal):
    row = lax.broadcasted_iota(jnp.int32, (TOKENS, TOKENS), 0)
    col = lax.broadcasted_iota(jnp.int32, (TOKENS, TOKENS), 1)
    if temporal:
        return (row & 1) == (col & 1)
    return (row >> 6) == (col >> 6)

def natural_from_sent():
    nat = lax.broadcasted_iota(jnp.int32, (TOKENS, TOKENS), 0)
    sent = lax.broadcasted_iota(jnp.int32, (TOKENS, TOKENS), 1)
    goes = ((sent >> 1) & 1) * 64 + (sent >> 2) * 2 + (sent & 1)
    return jnp.where(nat == goes, 1.0, 0.0).astype(BF16)

class Tiles:
    def __init__(self, ref, offset, scale=None):
        self.ref, self.offset, self.scale, self.pending = ref, offset, scale, None

    def add(self, head, value):
        low, high = window(head)
        for tile in range(low, high, LANES):
            part = value[:, tile - low : tile - low + LANES]
            if E * head > tile:
                part = self.pending + part
            if E * head + E >= tile + LANES:
                if self.scale is not None:
                    part = part * self.scale
                at = self.offset + tile
                self.ref[:, at : at + LANES] = part.astype(self.ref.dtype)
            else:
                self.pending = part

def attend_heads(temporal, x_ref, mix_ref, probs_ref):
    same = same_sequence(temporal)
    out = Tiles(mix_ref, 0)
    for head in range(HEADS):
        low, high = window(head)
        mask = head_mask(head, low, high)
        queries = x_ref[:, low:high]
        keys = x_ref[:, D + low : D + high] * mask
        values = x_ref[:, 2 * D + low : 2 * D + high] * mask
        scores = jnp.where(same, mul(queries, keys, NT) * SCALING, -1e30)
        powers = jnp.exp(scores - jnp.max(scores, axis=1, keepdims=True))
        probs = powers / jnp.sum(powers, axis=1, keepdims=True)
        probs_ref[head] = probs
        out.add(head, mul(probs.astype(BF16), values, NN))

ROWS = jax.ShapeDtypeStruct((TOKENS, D), BF16)
PROBS = jax.ShapeDtypeStruct((HEADS, TOKENS, TOKENS), F32)

def sent_rows(width):
    return jax.ShapeDtypeStruct((32, 4, width), BF16)

def specs(**places):
    kinds = {"smem": pltpu.SMEM, "vmem": pltpu.VMEM, "any": pl.ANY}
    return [pl.BlockSpec(memory_space=kinds[k]) for k, n in places.items() for _ in range(n)]

def call(kernel, out_shape, in_specs, scratch, name, micros=3, out_specs=None, vmem=VMEM_BYTES):
    return pl.pallas_call(
        kernel,
        out_shape=out_shape,
        in_specs=in_specs,
        **({} if out_specs is None else {"out_specs": out_specs}),
        scratch_shapes=scratch,
        cost_estimate=pl.CostEstimate(flops=micros * 10**9, bytes_accessed=1, transcendentals=0),
        compiler_params=pltpu.CompilerParams(vmem_limit_bytes=vmem),
        name=name,
    )

def attend_space(x):
    kernel = functools.partial(attend_heads, False)
    return call(kernel, (ROWS, PROBS), specs(vmem=1), [], "attend_space", 14)(x)


def unit_rows(place_ref):
    at_y, at_z = place_ref[2], place_ref[3]
    natural = lax.broadcasted_iota(jnp.int32, (288, 288), 0)
    unit = lax.broadcasted_iota(jnp.int32, (1, 288), 1)
    block = (unit * 1821) >> 16
    from_z = (at_z + (((block >> 1) + at_y) & 3) + 4 * (block & 1)) & 7
    return jnp.where(natural == from_z * 36 + (unit - block * 36), 1.0, 0.0).astype(BF16)


def stack_kernel(place_ref, *refs):
    *block_refs, out_ref, units = refs
    for a, ref in enumerate(block_refs):
        units[72 * a : 72 * a + 72] = ref[...]
    out_ref[...] = mul(unit_rows(place_ref), units[...], NN).astype(BF16)


def stack(place, blocks):
    out = jax.ShapeDtypeStruct((288, D), BF16)
    scratch = [pltpu.VMEM((288, D), BF16)]
    return call(stack_kernel, out, specs(smem=1, vmem=4), scratch, "stack", 1, vmem=32 * 1024 * 1024)(place, *blocks)


def attend_time_kernel(x_ref, mix_ref, probs_ref, x, mix):
    x[...] = x_ref[...].reshape(TOKENS, 3 * D)
    attend_heads(True, x, mix, probs_ref)
    mix_ref[...] = mix[...].reshape(32, 4, D)

def attend_time(x):
    scratch = [pltpu.VMEM((TOKENS, 3 * D), BF16), pltpu.VMEM((TOKENS, D), BF16)]
    return call(attend_time_kernel, (sent_rows(D), PROBS), specs(vmem=1), scratch, "attend_time")(x)

def send_kernel(x_ref, out_ref):
    out_ref[...] = mul(natural_from_sent(), x_ref[...], TN).astype(BF16).reshape(32, 4, 3 * D)

def send(x):
    return call(send_kernel, sent_rows(3 * D), specs(vmem=1), [], "send_order", vmem=32 * 1024 * 1024)(x)

def receive_kernel(x_ref, out_ref):
    x = x_ref[...].reshape(TOKENS, 3 * D)
    out_ref[...] = mul(natural_from_sent(), x, NN).astype(BF16)

def receive(x):
    out = jax.ShapeDtypeStruct((TOKENS, 3 * D), BF16)
    return call(receive_kernel, out, specs(vmem=1), [], "natural_order", vmem=32 * 1024 * 1024)(x)

def attend_back_heads(inv, x_ref, probs_ref, grad_ref, out_ref):
    query_out = Tiles(out_ref, 0)
    key_out = Tiles(out_ref, D)
    value_out = Tiles(out_ref, 2 * D, inv)
    for head in range(HEADS):
        low, high = window(head)
        mask = head_mask(head, low, high)
        queries = x_ref[:, low:high] * mask
        keys = x_ref[:, D + low : D + high] * mask
        values = x_ref[:, 2 * D + low : 2 * D + high]
        grads = grad_ref[:, low:high] * mask
        probs = probs_ref[head]
        value_out.add(head, mul(probs.astype(BF16), grads, TN))
        prob_grad = mul(grads, values, NT)
        inner = jnp.sum(prob_grad * probs, axis=1, keepdims=True)
        score_grad = (probs * (prob_grad - inner) * (SCALING * inv)).astype(BF16)
        query_out.add(head, mul(score_grad, keys, NN))
        key_out.add(head, mul(score_grad, queries, TN))

def attend_back_time_kernel(x_ref, probs_ref, grad_ref, out_ref, spread_ref, x, grad, out):
    x[...] = x_ref[...].reshape(TOKENS, 3 * D)
    grad[...] = grad_ref[:, :, :D].reshape(TOKENS, D)
    total = 0.25 * jnp.sum(grad_ref[:, :, D:].reshape(TOKENS, LANES).astype(F32))
    spread = jnp.sqrt(jnp.full((8, LANES), total, F32) / CELLS + HUBER_DELTA**2)
    spread_ref[...] = spread
    inv = 1.0 / spread[0:1, 0:1]
    attend_back_heads(inv, x, probs_ref, grad, out)
    out_ref[...] = out[...].reshape(32, 4, 3 * D)

def attend_back_time(x, probs, grad):
    wide = pltpu.VMEM((TOKENS, 3 * D), BF16)
    return call(
        attend_back_time_kernel,
        (sent_rows(3 * D), jax.ShapeDtypeStruct((8, LANES), F32)),
        specs(vmem=3),
        [wide, pltpu.VMEM((TOKENS, D), BF16), wide],
        "attend_back_time",
        5,
    )(x, probs, grad)

def attend_back_space_kernel(x_ref, probs_ref, grad_ref, spread_ref, out_ref):
    attend_back_heads(1.0 / spread_ref[0:1, 0:1], x_ref, probs_ref, grad_ref, out_ref)

def attend_back_space(x, probs, grad, spread):
    return call(
        attend_back_space_kernel,
        jax.ShapeDtypeStruct((TOKENS, 3 * D), BF16),
        specs(vmem=4),
        [],
        "attend_back_space",
        1,
        vmem=32 * 1024 * 1024,
    )(x, probs, grad, spread)

def fetch_weights(at_x, refs, weight, sems):
    copies = []
    for b in range(4):
        rows = pl.ds(pl.multiple_of(((at_x + b) & 3) * 288, 288), 288)
        copy = pltpu.make_async_copy(refs[b], weight.at[rows], sems.at[b])
        copy.start()
        copies.append(copy)
    return copies


def column_block(mix, index):
    blocks = [mix[:, 288 * q : 288 * q + 288] for q in range(4)]
    low = jnp.where(index == 0, blocks[0], blocks[1])
    high = jnp.where(index == 2, blocks[2], blocks[3])
    return jnp.where(index < 2, low, high)


def project_kernel(place_ref, time_ref, hidden_any, target_any, space_any, *rest):
    own_refs, other_refs = rest[0:4], rest[4:8]
    time_grad_ref, pack_refs = rest[8], rest[9:13]
    weights, hidden_ref, target_ref, space_ref, packs, sems = rest[13:]
    at_x, at_core = place_ref[0], place_ref[1]
    loads = [
        pltpu.make_async_copy(source, place, sems.at[2, n])
        for n, (source, place) in enumerate(
            ((hidden_any, hidden_ref), (target_any, target_ref), (space_any, space_ref))
        )
    ]
    for copy in loads:
        copy.start()
    copies = fetch_weights(at_x, own_refs, weights.at[at_core], sems.at[0])
    copies += fetch_weights(at_x, other_refs, weights.at[1 - at_core], sems.at[1])
    natural = natural_from_sent()
    for copy in loads:
        copy.wait()
    time_mix = mul(natural, time_ref[...].reshape(TOKENS, D), NN).astype(BF16)
    base = hidden_ref[...].astype(F32) - target_ref[...].astype(F32)
    first = at_core == 0
    space_mix = space_ref[...]
    for copy in copies[:4]:
        copy.wait()
    resid = base + mul(jnp.where(first, space_mix, time_mix), weights[at_core], NN)
    for copy in copies[4:]:
        copy.wait()
    resid = resid + mul(jnp.where(first, time_mix, space_mix), weights[1 - at_core], NN)
    total = jnp.sum(resid * resid)
    out_grad = resid.astype(BF16)
    time_grad = mul(out_grad, weights[1], NT).astype(BF16)
    time_grad = mul(natural, time_grad, TN).astype(BF16)
    lane = lax.broadcasted_iota(jnp.int32, (TOKENS, LANES), 1)
    whole = jnp.full((TOKENS, LANES), total, F32)
    first = whole.astype(BF16).astype(F32)
    second = (whole - first).astype(BF16).astype(F32)
    third = whole - first - second
    parts = jnp.where(lane == 0, first, jnp.where(lane == 1, second, jnp.where(lane == 2, third, 0.0)))
    time_grad_ref[:, :, :D] = time_grad.reshape(32, 4, D)
    time_grad_ref[:, :, D:] = parts.astype(BF16).reshape(32, 4, LANES)
    stores = []
    for a in range(4):
        packs[a, :, :D] = out_grad
        index = (at_x + a) & 3
        packs[a, :, D:] = jnp.concatenate(
            [column_block(space_mix, index), column_block(time_mix, index)], axis=1
        )
        stores.append(pltpu.make_async_copy(packs.at[a], pack_refs[a], sems.at[3, a]))
        stores[-1].start()
    for copy in stores:
        copy.wait()

def project(place, hidden, target, space_mix, time_mix, own, other):
    packed = jax.ShapeDtypeStruct((TOKENS, D + 576), BF16)
    return call(
        project_kernel,
        (sent_rows(D + LANES),) + (packed,) * 4,
        specs(smem=1, vmem=1, any=11),
        [pltpu.VMEM((2, D, D), BF16)]
        + [pltpu.VMEM((TOKENS, D), BF16)] * 3
        + [
            pltpu.VMEM((4, TOKENS, D + 576), BF16),
            pltpu.SemaphoreType.DMA((4, 4)),
        ],
        "project",
        8,
        specs(vmem=1, any=4),
    )(place, time_mix, hidden, target, space_mix, *own, *other)

def space_back_kernel(place_ref, pack_ref, *rest):
    own_refs, other_refs = rest[0:4], rest[4:8]
    out_ref, weight, sems = rest[8:]
    first = place_ref[1] == 0

    @pl.when(first)
    def _():
        for copy in fetch_weights(place_ref[0], own_refs, weight, sems):
            copy.wait()

    @pl.when(jnp.logical_not(first))
    def _():
        for copy in fetch_weights(place_ref[0], other_refs, weight, sems):
            copy.wait()

    out_ref[...] = mul(pack_ref[:, :D], weight[...], NT).astype(BF16)

def space_back(place, packed, own, other):
    scratch = [pltpu.VMEM((D, D), BF16), pltpu.SemaphoreType.DMA((4,))]
    return call(
        space_back_kernel, ROWS, specs(smem=1, vmem=1, any=8), scratch, "space_back", 3
    )(place, packed, *own, *other)

def weight_kernel(place_ref, *rest):
    spread_refs, pack_refs = rest[0:2], rest[2:10]
    out_refs, total = rest[10:14], rest[14]
    first = place_ref[1] == 0
    for n, pack_ref in enumerate(pack_refs):
        inv = 1.0 / spread_refs[n // 4][0:1, 0:1]
        out_grad = (pack_ref[:, :D].astype(F32) * inv).astype(BF16)
        mix = jnp.where(first, pack_ref[:, D : D + 288], pack_ref[:, D + 288 :])
        term = mul(mix, out_grad, TN)
        if n == 0:
            total[...] = term
        else:
            total[...] += term
    units = mul(unit_rows(place_ref), total[...].astype(BF16), TN).astype(BF16)
    for a in range(4):
        out_refs[a][...] = units[72 * a : 72 * a + 72]

def weight_grad(place, spreads, packs):
    return call(
        weight_kernel,
        (jax.ShapeDtypeStruct((72, D), BF16),) * 4,
        specs(smem=1, vmem=10),
        [pltpu.VMEM((288, D), F32)],
        "weight_grad",
        8,
        vmem=32 * 1024 * 1024,
    )(place, *spreads, *packs)

def halves_kernel(*refs):
    *block_refs, first_ref, second_ref = refs
    total = sum(ref[...].astype(F32) for ref in block_refs)
    first_ref[...] = total[:36].astype(BF16)
    second_ref[...] = total[36:].astype(BF16)

def halves(blocks):
    out = jax.ShapeDtypeStruct((36, D), BF16)
    return call(halves_kernel, (out, out), specs(vmem=4), [], "halves", 0, vmem=32 * 1024 * 1024)(*blocks)

def finish_kernel(place_ref, own_ref, other_ref, space_ref, time_ref):
    own, other = own_ref[...].astype(F32), other_ref[...].astype(F32)
    first = place_ref[1] == 0
    space_ref[...] = jnp.where(first, own, other)
    time_ref[...] = jnp.where(first, other, own)

def finish(place, own, other):
    rows = jax.ShapeDtypeStruct((36, D), F32)
    return call(finish_kernel, (rows, rows), specs(smem=1, vmem=2), [], "finish", vmem=32 * 1024 * 1024)(place, own, other)

def shift_z(value, slope, extra):
    extra = extra if slope > 0 else -extra
    pairs = [(8 * y + z, 8 * y + (z + slope * y + extra) % 8) for y in range(4) for z in range(8)]
    return lax.ppermute(value, ("y", "z"), pairs)

def shift(value, axis, size, step):
    return lax.ppermute(value, axis, [(i, (i + step) % size) for i in range(size)])

def swap(value):
    return lax.ppermute(value, "core", [(0, 1), (1, 0)])

def after(*values):
    return lax.optimization_barrier(values)

def add(blocks):
    return sum(block.astype(F32) for block in blocks).astype(BF16)

def exchange(value, axis):
    return lax.all_to_all(value, axis, split_axis=0, concat_axis=0, tiled=True)

def per_device(hidden_in, spatial_qkv, temporal_qkv, teacher_target, spatial_proj, temporal_proj):
    at_x, at_core, at_y, at_z = (lax.axis_index(a) for a in ("x", "core", "y", "z"))
    place = jnp.stack([at_x, at_core, at_y, at_z]).astype(jnp.int32)

    rows = jnp.where(at_core == 0, spatial_proj, temporal_proj)
    by_z = jnp.concatenate([shift_z(rows, -1, 0), shift_z(rows, -1, 4)])
    time_x = exchange(send(temporal_qkv.reshape(TOKENS, 3 * D)), SEQ)
    by_y = stack(place, [by_z] + [shift(by_z, "y", 4, 4 - a) for a in range(1, 4)])

    by_y, spatial_qkv = after(by_y, spatial_qkv)
    space_x = spatial_qkv.reshape(TOKENS, 3 * D)
    space_mix, space_probs = attend_space(space_x)
    time_x, space_mix, space_probs = after(time_x, space_mix, space_probs)
    time_mix, time_probs = attend_time(time_x)
    time_mix = exchange(time_mix, SEQ)
    own = [by_y] + [shift(by_y, "x", 4, 4 - b) for b in range(1, 4)]
    other = [swap(own[0])]
    time_mix, own[1], own[2], own[3] = after(time_mix, own[1], own[2], own[3])
    other += [swap(block) for block in own[1:]]

    time_grad, *packs = project(
        place,
        hidden_in.reshape(TOKENS, D),
        teacher_target.reshape(TOKENS, D),
        space_mix,
        time_mix,
        own,
        other,
    )
    time_back = exchange(time_grad, SEQ)
    space_grad = space_back(place, packs[0], own, other)
    packs = [packs[0]] + [shift(packs[b], "x", 4, b) for b in range(1, 4)]
    time_back, space_grad = after(time_back, space_grad)
    time_out, spread = attend_back_time(time_x, time_probs, time_back)
    clip_loss = spread[0, :1] - HUBER_DELTA
    _, spread, packs = after(time_out, spread, packs)
    spreads = [spread, swap(spread)]
    time_out = exchange(time_out, SEQ)
    packs = packs + [swap(block) for block in packs]

    spatial_qkv_grad = attend_back_space(space_x, space_probs, space_grad, spread)

    partial = weight_grad(place, spreads, packs)
    partial = halves([partial[0]] + [shift(partial[a], "y", 4, a) for a in range(1, 4)])
    partial, time_out, spatial_qkv_grad = after(partial, time_out, spatial_qkv_grad)
    piece = add([shift_z(partial[0], 1, 0), shift_z(partial[1], 1, 4)])
    ends = [shift(piece, "y", 4, a).astype(F32) for a in range(1, 4)]
    final = ((piece.astype(F32) + ends[1]) + (ends[0] + ends[2])).astype(BF16)
    spatial_proj_grad, temporal_proj_grad = finish(place, final, swap(final))
    temporal_qkv_grad = receive(time_out)
    return (
        clip_loss,
        spatial_qkv_grad.reshape(1, 2, 64, 3 * D),
        temporal_qkv_grad.reshape(1, 2, 64, 3 * D),
        spatial_proj_grad,
        temporal_proj_grad,
    )

def solution(mesh):
    fine = Mesh(mesh.devices.reshape(4, 2, 4, 8), ("y", "core", "x", "z"))
    clips = P(DP, SEQ, None, None)
    weight = P(SEQ, None)
    return jax.shard_map(
        per_device,
        mesh=fine,
        in_specs=(clips, clips, clips, clips, weight, weight),
        out_specs=(P(DP), clips, clips, weight, weight),
        check_vma=False,
    )
```
